128 devices in a mesh: span: 8 (over x, core), cnn: 16 (over z, y).
Axes of the slice: x: 4, y: 4, z: 4, core: 2. Of those that a mesh axis runs over, the one named last changes fastest.
Arguments:
- views: bfloat16 [1024, 4, 4, 128, 256], P(('span', 'cnn')), may hold values from -11 to 11
- live_counts: int32 [8, 16], P('span', 'cnn'), may hold values from 1 to 8, 32 in all within a row
- skeleton_edges: int32 [1024, 4], P(('span', 'cnn')), may hold values from 0 to 11
- boundary_rows: int32 [256], P(('span', 'cnn')), may hold values from 0 to 7
- patch_weight: bfloat16 [4, 4, 4, 128], replicated, may hold values from -1 to 1
- conv_first: bfloat16 [3, 3, 128, 128], replicated, may hold values from -0.25 to 0.25
- conv_second: bfloat16 [3, 3, 128, 128], replicated, may hold values from -0.25 to 0.25
- conv_third: bfloat16 [3, 3, 128, 256], replicated, may hold values from -0.25 to 0.25
- conv_fourth: bfloat16 [3, 3, 256, 256], replicated, may hold values from -0.1875 to 0.1875
- head_weight: float32 [256, 7], replicated, may hold values from -1.5 to 1.5
Outputs:
- labels: float32 [1024, 7], P(('span', 'cnn'))
The draws below stay inside these ranges and needn't reach their ends.
Inputs may be any that keep to these rules, and one draw needn't show every extreme that they name: `live_counts`: in each span the 16 counts sum to 32 and the largest is exactly 8. `skeleton_edges`: an entry below 4 names an exported row of a neighbouring span, any other a location of the own device.
All inputs are finite; a program needn't handle non-finite values. No bound on the sum of `live_counts` on one device may be relied on, other than what follows from the above.
Results may differ from the reference program's by a relative error of at most 0.0004.
Values may be sent and summed in bfloat16 or wider, within the bound.
A program may use at most 128 MiB of HBM per device.

```python
import math
import jax
import jax.numpy as jnp
import numpy as np
from jax import lax

VIEWS = 4
CH = 4
H = 128
W = 256
PATCH = 4
C1 = 128
C2 = 256
CLS = 7
LOC_DEV = 8
BAL = 2
RIM = 2
DEGREE = 4
ITERS = 2
LOCS = 1024
BOUNDS = 256
N_SPAN = 8
N_CNN = 16


def draw_views(key, part):
    key = jax.random.fold_in(key, 11)
    noise_key, centre_key, scale_key = jax.random.split(key, 3)
    full_shape = (LOCS, VIEWS, CH, H, W)
    lead_shape = (LOCS, VIEWS, CH, 1, 1)
    centre = jax.random.uniform(centre_key, lead_shape, jnp.float32, -1.0, 1.0)
    spread = jnp.exp(jax.random.uniform(scale_key, lead_shape, jnp.float32, math.log(0.25), math.log(2.0)))
    noise_values = jnp.clip(jax.random.normal(noise_key, full_shape, jnp.float32), -5.0, 5.0)
    return (centre + spread * noise_values).astype(jnp.bfloat16)


def plant(drawn, key, smallest, largest):
    index_at = [jax.random.randint(jax.random.fold_in(key, axis), (), 0, length) for axis, length in enumerate(drawn.shape)]
    longest = drawn.shape.index(max(drawn.shape))
    next_to = index_at[:longest] + [(index_at[longest] + 1) % drawn.shape[longest]] + index_at[longest + 1:]
    return drawn.at[tuple(index_at)].set(smallest).at[tuple(next_to)].set(largest)


def profile(count, total, most, lean):
    portions = [(1 << 20) // math.isqrt(grade ** lean) + 1 for grade in range(2, count + 1)]
    surplus, counts = total - most - (count - 1), [1] * (count - 1)
    while surplus > 0:
        candidates = [i for i in range(count - 1) if counts[i] < most]
        mass, left = sum([portions[i] for i in candidates]), surplus
        for i in candidates:
            extra = min(most - counts[i], max(1, left * portions[i] // mass), surplus)
            counts[i] = counts[i] + extra
            surplus = surplus - extra
    return np.array([most] + counts)


def ragged_sizes(rng, count, total, limit, lean):
    if count == 2:
        one = jax.random.randint(rng, (), max(1, total - limit), min(limit, total - 1) + 1)
        return jnp.stack([one, total - one])
    sizes = jnp.asarray(profile(count, total, limit, lean), jnp.int32)
    twos = (count - 1) // 2
    giver, taker = sizes[1:1 + 2 * twos:2], sizes[2:2 + 2 * twos:2]
    room = jnp.minimum(giver - 1, limit - taker)
    passed = jax.random.randint(jax.random.fold_in(rng, 1), (twos,), 0, 1 << 20) % (room + 1)
    sizes = sizes.at[1:1 + 2 * twos:2].set(giver - passed).at[2:2 + 2 * twos:2].set(taker + passed)
    return sizes[jax.random.permutation(jax.random.fold_in(rng, 2), count)]


def bell_draw(key, dims, scale, most, kind=jnp.bfloat16):
    array = scale * jax.random.normal(key, dims, jnp.float32)
    return jnp.clip(array, min=-most, max=most).astype(kind)


def setup_inputs(seed: int = 0) -> dict:
    key_list = jax.random.split(jax.random.key(seed), 11)
    return {
        "views": draw_views(jax.random.fold_in(key_list[10], 71), 0),
        "live_counts": jax.vmap(lambda own: ragged_sizes(own, N_CNN, BAL * N_CNN, LOC_DEV, 2))(jax.random.split(key_list[1], N_SPAN)).reshape((N_SPAN, N_CNN)).astype(jnp.int32),
        "skeleton_edges": plant(jax.random.randint(key_list[2], (LOCS, DEGREE), 0, LOC_DEV + 2 * RIM), jax.random.fold_in(key_list[2], 1), 0, (LOC_DEV + 2 * RIM) - 1).astype(jnp.int32),
        "boundary_rows": plant(jax.random.randint(key_list[3], (BOUNDS,), 0, LOC_DEV), jax.random.fold_in(key_list[3], 1), 0, LOC_DEV - 1).astype(jnp.int32),
        "patch_weight": bell_draw(key_list[4], (PATCH, PATCH, CH, C1), (PATCH * PATCH * CH // 2) ** -0.5, 1.0),
        "conv_first": bell_draw(key_list[5], (3, 3, C1, C1), (9 * C1 // 2) ** -0.5, 0.25),
        "conv_second": bell_draw(key_list[6], (3, 3, C1, C1), (9 * C1 // 2) ** -0.5, 0.25),
        "conv_third": bell_draw(key_list[7], (3, 3, C1, C2), (9 * C1 // 2) ** -0.5, 0.25),
        "conv_fourth": bell_draw(key_list[8], (3, 3, C2, C2), (9 * C2 // 2) ** -0.5, 0.1875),
        "head_weight": bell_draw(key_list[9], (C2, CLS), 0.25, 1.5, jnp.float32),
    }


LAMBDA_MIX = 0.5
TILE_LAYOUT = ("NCHW", "HWIO", "NHWC")
CONV_LAYOUT = ("NHWC", "HWIO", "NHWC")


def convolve(inputs, kernel, strides, padding_mode, layout):
    return lax.conv_general_dilated(inputs.astype(jnp.float32), kernel.astype(jnp.float32), strides, padding_mode, dimension_numbers=layout, precision=lax.Precision.HIGHEST)


def network(batch, weights):
    embedded = convolve(batch, weights[0], (PATCH, PATCH), "VALID", TILE_LAYOUT)
    first_map = jax.nn.relu(embedded).astype(jnp.bfloat16)
    raised = jax.nn.relu(convolve(first_map, weights[1], (1, 1), "SAME", CONV_LAYOUT))
    batch_size, map_rows, map_cols, channels = raised.shape
    pooled = raised.reshape(batch_size, map_rows // 2, 2, map_cols // 2, 2, channels).mean(axis=(2, 4)).astype(jnp.bfloat16)
    third_map = jax.nn.relu(convolve(pooled, weights[2], (1, 1), "SAME", CONV_LAYOUT)).astype(jnp.bfloat16)
    fourth_map = jax.nn.relu(convolve(third_map, weights[3], (1, 1), "SAME", CONV_LAYOUT)).astype(jnp.bfloat16)
    fifth_map = jax.nn.relu(convolve(fourth_map, weights[4], (1, 1), "SAME", CONV_LAYOUT))
    feature = jnp.mean(fifth_map, axis=(1, 2))
    return jnp.dot(feature, weights[5], preferred_element_type=jnp.float32, precision=lax.Precision.HIGHEST)


def reference(views, live_counts, skeleton_edges, boundary_rows, patch_weight, conv_first, conv_second, conv_third, conv_fourth, head_weight):
    groups = N_SPAN * N_CNN
    weights = (patch_weight, conv_first, conv_second, conv_third, conv_fourth, head_weight)
    counts_flat = live_counts.reshape(groups).astype(jnp.int32)
    ends_rank = jnp.cumsum(live_counts, axis=1).astype(jnp.int32)
    starts_rank = ends_rank - live_counts.astype(jnp.int32)
    ranks = jnp.arange(BAL * N_CNN, dtype=jnp.int32)
    owners = jnp.sum((ends_rank[:, None, :] <= ranks[None, :, None]).astype(jnp.int32), axis=2)
    offsets = ranks[None, :] - jnp.take_along_axis(starts_rank, owners, axis=1)
    span_ids = jnp.arange(N_SPAN, dtype=jnp.int32)[:, None]
    location_ids = ((span_ids * N_CNN + owners) * LOC_DEV + offsets).astype(jnp.int32).reshape(-1, BAL)

    def label_block(block_ids):
        batch = views[block_ids].reshape((BAL * VIEWS, CH, H, W))
        return network(batch, weights).reshape(BAL, VIEWS, CLS)

    view_logits = lax.map(label_block, location_ids)
    located = jnp.mean(view_logits, axis=2).reshape(-1, CLS)
    smooth = jnp.zeros((LOCS, CLS), jnp.float32).at[location_ids.reshape(-1)].set(located)
    smooth = smooth.reshape(groups, LOC_DEV, CLS)
    alive_mask = (jnp.arange(LOC_DEV, dtype=jnp.int32)[None, :] < counts_flat[:, None]).astype(jnp.float32)[:, :, None]
    exported_ids = boundary_rows.reshape(groups, RIM).astype(jnp.int32) % counts_flat[:, None]
    edge_ids = skeleton_edges.reshape(groups, LOC_DEV * DEGREE).astype(jnp.int32)
    border = 2 * RIM
    lookup = jnp.where(edge_ids < border, edge_ids, border + (edge_ids - border) % counts_flat[:, None])
    for iteration in range(ITERS):
        exported = jnp.take_along_axis(smooth, exported_ids[:, :, None], axis=1).reshape(N_SPAN, N_CNN, RIM, CLS)
        blank = jnp.zeros((1, N_CNN, RIM, CLS), jnp.float32)
        from_below = jnp.concatenate([blank, exported[:-1]], axis=0).reshape(groups, RIM, CLS)
        from_above = jnp.concatenate([exported[1:], blank], axis=0).reshape(groups, RIM, CLS)
        row_table = jnp.concatenate([from_below, from_above, smooth], axis=1)
        neighbours = jnp.take_along_axis(row_table, lookup[:, :, None], axis=1).reshape(groups, LOC_DEV, DEGREE, CLS)
        smooth = ((1.0 - LAMBDA_MIX) * smooth + LAMBDA_MIX * jnp.mean(neighbours, axis=2)) * alive_mask
    return smooth.reshape(LOCS, CLS)
```

```python
import functools

import jax
import jax.numpy as jnp
from jax import lax
from jax.experimental import pallas as pl
from jax.experimental.pallas import tpu as pltpu
from jax.sharding import PartitionSpec as P

BF = jnp.bfloat16
F32 = jnp.float32
I32 = jnp.int32
MESH = pl.DeviceIdType.MESH
VMEM = pl.BlockSpec(memory_space=pltpu.VMEM)
SMEM = pl.BlockSpec(memory_space=pltpu.SMEM)
ANY = pl.BlockSpec(memory_space=pl.ANY)

VIEWS = 4
SLOTS = 8
RIM = 2
DEGREE = 4
ITERS = 2
CLASSES = 7
PAIR = 2
DIRS = 7
BACK = (0, 2, 1, 4, 3, 6, 5)
GOAL = 3
MOST = (2, 1)
ROUNDS = 4
OWN = DIRS - 1
OWN_LATE = OWN + SLOTS - 1
PLACES = DIRS + 2 * (SLOTS - 1)
FULL = (0, 256)


def dot(a, b):
    return jnp.dot(a, b, preferred_element_type=F32)


def rows_down(x):
    group = lax.broadcasted_iota(I32, x.shape, 0) % 16
    return jnp.where(group == 0, 0.0, pltpu.roll(x, 1, 0))


def rows_up(x):
    group = lax.broadcasted_iota(I32, x.shape, 0) % 16
    return jnp.where(group == 15, 0.0, pltpu.roll(x, x.shape[0] - 1, 0))


def prepare(patch_w, w1, w2, sel, wp, w1p, w2p, *maps):
    row = lax.broadcasted_iota(I32, (256, 256), 0)
    col = lax.broadcasted_iota(I32, (256, 256), 1)
    want = 16 * (row % 16) + 4 * ((row // 16) % 4) + row // 64
    sel[...] = jnp.where(col == want, 1.0, 0.0).astype(BF)
    row = lax.broadcasted_iota(I32, (512, 64), 0)
    col = lax.broadcasted_iota(I32, (512, 64), 1)
    dx, ch, dy = row // 128, (row // 32) % 4, row % 4
    spread = dot(jnp.where(col == dy * 16 + dx * 4 + ch, 1.0, 0.0).astype(BF), patch_w[...])
    r_of = (lax.broadcasted_iota(I32, (512, 128), 0) % 32) // 4
    for r in range(8):
        wp[:, r * 128 : (r + 1) * 128] = jnp.where(r_of == r, spread, 0.0).astype(BF)
    zero = jnp.zeros((128, 128), BF)
    for w, out in ((w1, w1p), (w2, w2p)):
        for dy in range(3):
            base = dy * 512
            for i, (even, odd) in enumerate(((1, 0), (2, 1), (0, None), (None, 2))):
                rows = pl.ds(base + i * 128, 128)
                out[rows, 0:128] = zero if even is None else w[dy, even]
                out[rows, 128:256] = zero if odd is None else w[dy, odd]
    for ref in maps:
        last = ref.shape[1] - 1
        for n in range(ref.shape[0]):
            ref[n, 0] = jnp.zeros(ref.shape[2:], BF)
            ref[n, last] = jnp.zeros(ref.shape[2:], BF)


def taps(parts, first, rows):
    pieces = []
    for dy in range(3):
        for ref, lanes in parts:
            piece = ref[pl.ds(first + dy, rows), :, lanes[0] : lanes[1]]
            pieces.append(piece.reshape(rows * piece.shape[1], piece.shape[2]))
    return jnp.concatenate(pieces, axis=1)


def tile_stage(load, sel, wp, xc, xs):
    pixels = jnp.concatenate([load(ch, 32 * b, 32) for b in range(4) for ch in range(4)], axis=0)
    moved = lax.dot_general(
        sel[...], pixels, (((1,), (1,)), ((), ())), preferred_element_type=F32
    ).astype(BF)
    tiles = jnp.concatenate(
        [
            jnp.concatenate(
                [moved[dx * 64 : (dx + 1) * 64, b * 128 : (b + 1) * 128] for dx in range(4)], axis=1
            )
            for b in range(4)
        ],
        axis=0,
    )
    for n in range(4):
        out = jnp.maximum(dot(tiles, wp[:, n * 256 : (n + 1) * 256]), 0.0)
        for half in range(2):
            lanes = out[:, half * 128 : (half + 1) * 128]
            for b in range(4):
                r = 1 + b * 8 + n * 2 + half
                q = [lanes[b * 64 + i * 16 : b * 64 + (i + 1) * 16] for i in range(4)]
                qb = [v.astype(BF) for v in q]
                xc[r, 0:16, 0:128] = qb[0]
                xc[r, 0:16, 128:256] = qb[1]
                xc[r, 16:32, 0:128] = qb[2]
                xc[r, 16:32, 128:256] = qb[3]
                xs[r, 0:16, 0:128] = rows_down(q[3]).astype(BF)
                xs[r, 0:16, 128:256] = qb[2]
                xs[r, 16:32, 0:128] = qb[1]
                xs[r, 16:32, 128:256] = rows_up(q[0]).astype(BF)


def first_stage(chunk, w1p, xc, xs, yc, ys):
    out = jnp.maximum(dot(taps(((xc, FULL), (xs, FULL)), chunk * 8, 8), w1p[...]), 0.0)
    pooled = (out[:, 0:128] + out[:, 128:256]).reshape(4, 2, 32, 128)
    pooled = (pooled[:, 0] + pooled[:, 1]) * 0.25
    even, odd = pooled[:, 0:16], pooled[:, 16:32]
    rows = pl.ds(1 + chunk * 4, 4)
    yc[rows, :, 0:128] = even.astype(BF)
    yc[rows, :, 128:256] = odd.astype(BF)
    ys[rows, :, 0:128] = rows_down(odd.reshape(64, 128)).astype(BF).reshape(4, 16, 128)
    ys[rows, :, 128:256] = rows_up(even.reshape(64, 128)).astype(BF).reshape(4, 16, 128)


def second_stage(w2p, yc, ys, tc, ts):
    out = jnp.maximum(dot(taps(((yc, FULL), (ys, FULL)), 0, 16), w2p[...]), 0.0)
    tc[1:17] = out.astype(BF).reshape(16, 16, 256)
    ts[1:17, :, 0:128] = rows_down(out[:, 128:256]).astype(BF).reshape(16, 16, 128)
    ts[1:17, :, 128:256] = rows_up(out[:, 0:128]).astype(BF).reshape(16, 16, 128)


def third_stage(w3, tc, ts, fe, fo, fm, fp):
    even = jnp.maximum(dot(taps(((ts, (0, 128)), (tc, FULL)), 0, 16), w3[...]), 0.0)
    odd = jnp.maximum(dot(taps(((tc, FULL), (ts, (128, 256))), 0, 16), w3[...]), 0.0)
    fe[1:17] = even.astype(BF).reshape(16, 16, 256)
    fo[1:17] = odd.astype(BF).reshape(16, 16, 256)
    fm[1:17] = rows_down(odd).astype(BF).reshape(16, 16, 256)
    fp[1:17] = rows_up(even).astype(BF).reshape(16, 16, 256)


def fourth_stage(w4, fe, fo, fm, fp):
    even = jnp.maximum(dot(taps(((fm, FULL), (fe, FULL), (fo, FULL)), 0, 16), w4[...]), 0.0)
    odd = jnp.maximum(dot(taps(((fe, FULL), (fo, FULL), (fp, FULL)), 0, 16), w4[...]), 0.0)
    return jnp.sum(even + odd, axis=0, keepdims=True) * (1.0 / 512)


def pair_feature(loads, w3, w4, sel, wp, w1p, w2p, *maps):
    own = [[m.at[v] for m in maps] for v in range(PAIR)]
    for v in range(PAIR):
        tile_stage(loads[v], sel, wp, *own[v][0:2])
    for chunk in range(4):
        for v in range(PAIR):
            first_stage(chunk, w1p, *own[v][0:4])
    for v in range(PAIR):
        second_stage(w2p, *own[v][2:6])
    for v in range(PAIR):
        third_stage(w3, *own[v][4:10])
    features = [fourth_stage(w4, *own[v][6:10]) for v in range(PAIR)]
    return features[0] + features[1]


def net_scratch():
    shapes = [(256, 256), (512, 1024), (1536, 256), (1536, 256)]
    shapes += [(PAIR, 34, 32, 256)] * 2 + [(PAIR, 18, 16, 256)] * 8
    return [pltpu.VMEM(shape, BF) for shape in shapes]


def neighbours():
    s, c = lax.axis_index("span"), lax.axis_index("cnn")
    z, y = c // 4, c % 4
    return (
        (s + 1 - 2 * (s % 2), c),
        ((s + 2) % 8, c),
        ((s + 6) % 8, c),
        (s, (c + 4) % 16),
        (s, (c + 12) % 16),
        (s, z * 4 + (y + 1) % 4),
        (s, z * 4 + (y + 3) % 4),
    )


def seen(d, v):
    def ahead(n):
        return pltpu.roll(v, (128 - n) % 128, 1)

    g = lax.broadcasted_iota(I32, v.shape, 1)
    if d == 0:
        return jnp.where(g % 32 < 16, ahead(16), ahead(112))
    if d == 1:
        return ahead(32)
    if d == 2:
        return ahead(96)
    if d == 3:
        return jnp.where(g % 16 < 12, ahead(4), ahead(116))
    if d == 4:
        return jnp.where(g % 16 >= 4, ahead(124), ahead(12))
    if d == 5:
        return jnp.where(g % 4 < 3, ahead(1), ahead(125))
    return jnp.where(g % 4 >= 1, ahead(127), ahead(3))


def make_plan(counts):
    extra = counts - 1
    divisor = jnp.maximum(extra, 1)
    bit = []
    for d in range(DIRS):
        rest = jnp.full_like(counts, d)
        for _ in range(d):
            rest = jnp.where(rest >= divisor, rest - divisor, rest)
        bit.append(jnp.left_shift(jnp.ones_like(counts), 1 + rest))
    zero = jnp.zeros_like(counts)
    load = 2 * extra
    passed, taken, number = [zero, zero], [zero, zero], [zero, zero]
    for turn in range(ROUNDS):
        if turn:
            over = (load > GOAL).astype(I32)
            near = zero
            for d in range(DIRS):
                near = near | seen(d, over)
        for half in (0, 1) if turn % 2 == 0 else (1, 0):
            for d in range(DIRS) if turn % 2 == 0 else reversed(range(DIRS)):
                room = jnp.where((number[half] < MOST[half]) & (load < GOAL), load, 99)
                there = seen(d, room)
                wish = load > GOAL
                if turn:
                    wish = wish | ((load == GOAL) & (near > 0)) | (load - there >= 2)
                push = wish & (there < 99) & ((passed[half] & bit[d]) == 0) & (extra > 0)
                gone = push.astype(I32)
                come = seen(BACK[d], gone)
                passed[half] = passed[half] | (gone * bit[d])
                taken[half] = taken[half] | (come << BACK[d])
                number[half] = number[half] + come
                load = load - gone + come
    return passed, taken


def lowest(mask, places):
    place = jnp.int32(-1)
    for i in reversed(range(places)):
        place = jnp.where((mask >> i) & 1 == 1, jnp.int32(i), place)
    return place


def label_kernel(
    views, count, patch_w, w1, w2, w3, w4, head,
    total_out, left_out,
    own0, own_a, own_b, own_c, own_d, early, late, send, mine, x_in, c_mine, c_in, back_out, back_in,
    sel, wp, w1p, w2p, m0, m1, m2, m3, m4, m5, m6, m7, m8, m9,
    own_sem, local_sem, view_send, view_recv, x_send, x_recv, c_send, c_recv, b_send, b_recv,
):
    net = (sel, wp, w1p, w2p, m0, m1, m2, m3, m4, m5, m6, m7, m8, m9)
    s, c = lax.axis_index("span"), lax.axis_index("cnn")
    near = neighbours()
    along_x = [((s + o) % 8, c) for o in range(1, 8)]
    along_c = [(s, (c + o) % 16) for o in range(1, 16)]

    own_copy = pltpu.make_async_copy(views.at[0], own0, own_sem)
    own_copy.start()
    own = ((own_a, own_b), (own_c, own_d))
    copies = []
    for half in range(2):
        for j in range(PAIR):
            copies.append(
                pltpu.make_async_copy(
                    views.at[pl.ds(1, SLOTS - 1), half * PAIR + j], own[half][j], local_sem.at[half, j]
                )
            )
            copies[-1].start()

    barrier = pltpu.get_barrier_semaphore()
    for other in along_x + along_c:
        pl.semaphore_signal(barrier, inc=1, device_id=other, device_id_type=MESH)
    pl.semaphore_wait(barrier, len(along_x) + len(along_c))

    own_count = count[0, 0]
    me = s * 16 + c
    lane = lax.broadcasted_iota(I32, (8, 128), 1)
    mine[...] = jnp.where(lane == me, own_count, 0)
    x_copies = []
    for o in range(7):
        x_copies.append(
            pltpu.make_async_remote_copy(
                src_ref=mine, dst_ref=x_in.at[o], send_sem=x_send.at[o], recv_sem=x_recv.at[o],
                device_id=along_x[o], device_id_type=MESH,
            )
        )
        x_copies[-1].start()

    divisor = jnp.maximum(own_count - 1, 1)
    slot = [jnp.int32(1) + lax.rem(jnp.int32(d), divisor) for d in range(DIRS)]
    view_copies = [[], []]
    for half in range(2):
        for j in range(PAIR):
            copies[half * PAIR + j].wait()
            for d in range(DIRS):
                for ch in range(4):
                    send[half, j, d, ch] = own[half][j][jnp.clip(slot[d] - 1, 0, SLOTS - 2), ch]
                target = (early, late)[half].at[j, BACK[d]]
                copy = pltpu.make_async_remote_copy(
                    src_ref=send.at[half, j, d], dst_ref=target,
                    send_sem=view_send.at[half, j, d], recv_sem=view_recv.at[half, j, BACK[d]],
                    device_id=near[d], device_id_type=MESH,
                )
                copy.start()
                view_copies[half].append(copy)

    prepare(patch_w, w1, w2, *net)
    for copy in x_copies:
        copy.wait()
    total = mine[...]
    for o in range(7):
        total = total + x_in[o]
    c_mine[...] = total
    c_copies = []
    for o in range(15):
        c_copies.append(
            pltpu.make_async_remote_copy(
                src_ref=c_mine, dst_ref=c_in.at[o], send_sem=c_send.at[o], recv_sem=c_recv.at[o],
                device_id=along_c[o], device_id_type=MESH,
            )
        )
        c_copies[-1].start()

    own_copy.wait()

    def own_pair(half):
        loads = [
            lambda ch, first, rows, v=half * PAIR + j: own0[v, ch, pl.ds(first, rows), :]
            for j in range(PAIR)
        ]
        return pair_feature(loads, w3, w4, *net)

    units = [own_pair(0)]
    for copy in c_copies:
        copy.wait()
    counts = c_mine[...]
    for o in range(15):
        counts = counts + c_in[o]
    passed, taken = make_plan(counts)

    def here(v):
        return jnp.sum(jnp.where((lane == me)[0:1], v[0:1], 0))

    live = (jnp.left_shift(jnp.int32(1), own_count) - 1) & 254
    kept = [live & ~here(passed[half]) for half in range(2)]
    got = [here(taken[half]) for half in range(2)]
    units.append(own_pair(1))

    first_mask = got[0] | ((kept[0] >> 1) << DIRS) | ((kept[1] >> 1) << (OWN_LATE + 1))
    picks = []
    for _ in range(GOAL):
        pick = lowest(first_mask, PLACES)
        picks.append(pick)
        first_mask = first_mask & ~jnp.where(
            pick >= 0, jnp.left_shift(jnp.int32(1), jnp.maximum(pick, 0)), 0
        )
    late_dir = lowest(got[1], DIRS)
    has_late = late_dir >= 0
    third = picks[2]
    first_mask = first_mask | jnp.where(
        has_late & (third >= 0), jnp.left_shift(jnp.int32(1), jnp.maximum(third, 0)), 0
    )
    picks[2] = jnp.where(has_late, PLACES + late_dir, third)

    for copy in view_copies[0]:
        copy.wait()

    def at_place(place, j, ch, first, rows):
        pixels = [
            ref[jnp.clip(place - base, 0, DIRS - 1), ch, pl.ds(first, rows), :]
            for ref, base in ((early.at[j], 0), (own[0][j], OWN + 1), (own[1][j], OWN_LATE + 1))
        ]
        return jnp.where(
            place <= OWN, pixels[0], jnp.where(place <= OWN_LATE, pixels[1], pixels[2])
        )

    for n in range(GOAL - 1):
        loads = [
            lambda ch, first, rows, j=j, n=n: at_place(picks[n], j, ch, first, rows)
            for j in range(PAIR)
        ]
        units.append(pair_feature(loads, w3, w4, *net))
    for copy in view_copies[1]:
        copy.wait()
    place_late = jnp.clip(late_dir, 0, DIRS - 1)
    loads = [
        lambda ch, first, rows, j=j: jnp.where(
            has_late,
            late[j, place_late, ch, pl.ds(first, rows), :],
            at_place(third, j, ch, first, rows),
        )
        for j in range(PAIR)
    ]
    units.append(pair_feature(loads, w3, w4, *net))

    units = jnp.concatenate(units + [jnp.zeros((8 - len(units), 256), F32)], axis=0)
    logits = (
        jnp.dot(units, head[...], preferred_element_type=F32, precision=lax.Precision.HIGHEST)
        * (1.0 / VIEWS)
    )
    logits = jnp.concatenate([logits, jnp.zeros((8, 128 - CLASSES), F32)], axis=1)
    row = lax.broadcasted_iota(I32, (8, 128), 0)
    result = jnp.where(row == 0, logits[0:1] + logits[1:2], 0.0)
    for n, pick in enumerate(picks):
        unit = logits[2 + n : 3 + n]
        for own in (OWN, OWN_LATE):
            is_own = (pick >= own + 1) & (pick < own + SLOTS)
            result = result + jnp.where(is_own & (row == pick - own), unit, 0.0)
    b_copies = []
    for d in range(DIRS):
        answer = jnp.zeros((8, 128), F32)
        for n, pick in enumerate(picks):
            ours = (pick == d) | (pick == PLACES + d)
            answer = answer + jnp.where(ours, logits[2 + n : 3 + n], 0.0)
        back_out[d] = answer
        b_copies.append(
            pltpu.make_async_remote_copy(
                src_ref=back_out.at[d], dst_ref=back_in.at[BACK[d]],
                send_sem=b_send.at[d], recv_sem=b_recv.at[BACK[d]],
                device_id=near[d], device_id_type=MESH,
            )
        )
        b_copies[-1].start()
    rest0 = (first_mask >> DIRS) & 127
    rest1 = (first_mask >> (OWN_LATE + 1)) & 127
    left_out[...] = jnp.where(lane == 0, rest0 | (rest1 << 7), 0)
    for copy in b_copies:
        copy.wait()
    for d in range(DIRS):
        result = result + jnp.where(row == slot[d], back_in[d], 0.0)
    total_out[...] = result


def label(views, count, patch_w, w1, w2, w3, w4, head):
    dma = pltpu.SemaphoreType.DMA
    pixels = (4, 128, 256)
    tile = (8, 128)
    return pl.pallas_call(
        label_kernel,
        out_shape=(jax.ShapeDtypeStruct(tile, F32), jax.ShapeDtypeStruct(tile, I32)),
        in_specs=[ANY, SMEM] + [VMEM] * 6,
        out_specs=(VMEM, VMEM),
        scratch_shapes=[
            pltpu.VMEM((VIEWS, *pixels), BF),
            *[pltpu.VMEM((SLOTS - 1, *pixels), BF)] * (2 * PAIR),
            pltpu.VMEM((PAIR, DIRS, *pixels), BF),
            pltpu.VMEM((PAIR, DIRS, *pixels), BF),
            pltpu.VMEM((2, PAIR, DIRS, *pixels), BF),
            pltpu.VMEM(tile, I32),
            pltpu.VMEM((7, *tile), I32),
            pltpu.VMEM(tile, I32),
            pltpu.VMEM((15, *tile), I32),
            pltpu.VMEM((DIRS, *tile), F32),
            pltpu.VMEM((DIRS, *tile), F32),
            *net_scratch(),
            dma(()), dma((2, PAIR)),
            dma((2, PAIR, DIRS)), dma((2, PAIR, DIRS)),
            dma((7,)), dma((7,)), dma((15,)), dma((15,)), dma((DIRS,)), dma((DIRS,)),
        ],
        compiler_params=pltpu.CompilerParams(
            collective_id=0, has_side_effects=True, vmem_limit_bytes=58 << 20
        ),
    )(views, count, patch_w, w1, w2, w3, w4, head)


def rest_kernel(
    left, views, patch_w, w1, w2, w3, w4, head, total,
    total_out, own, pw_v, w1_v, w2_v, w3_v, w4_v, *net_and_sems,
):
    net, sems = net_and_sems[:-1], net_and_sems[-1]
    mask = left[0, 0]
    total_out[...] = total[...]

    @pl.when(mask != 0)
    def _():
        moves = [
            pltpu.make_async_copy(a, b, sems.at[i])
            for i, (a, b) in enumerate(
                ((patch_w, pw_v), (w1, w1_v), (w2, w2_v), (w3, w3_v), (w4, w4_v))
            )
        ]
        for move in moves:
            move.start()
        for move in moves:
            move.wait()
        prepare(pw_v, w1_v, w2_v, *net)

        @pl.loop(0, 2 * (SLOTS - 1))
        def _(i):
            @pl.when((mask >> i) & 1 == 1)
            def _():
                slot, half = 1 + i % (SLOTS - 1), i // (SLOTS - 1)
                move = pltpu.make_async_copy(
                    views.at[slot, pl.ds(half * PAIR, PAIR)], own, sems.at[5]
                )
                move.start()
                move.wait()
                loads = [
                    lambda ch, first, rows, v=j: own[v, ch, pl.ds(first, rows), :]
                    for j in range(PAIR)
                ]
                unit = jnp.broadcast_to(pair_feature(loads, w3_v, w4_v, *net), (8, 256))
                logits = (
                    jnp.dot(unit, head[...], preferred_element_type=F32, precision=lax.Precision.HIGHEST)
                    * (1.0 / VIEWS)
                )
                logits = jnp.concatenate([logits, jnp.zeros((8, 128 - CLASSES), F32)], axis=1)
                row = lax.broadcasted_iota(I32, (8, 128), 0)
                total_out[...] += jnp.where(row == slot, logits, 0.0)


def rest(left, views, patch_w, w1, w2, w3, w4, head, total):
    pixels = (4, 128, 256)
    return pl.pallas_call(
        rest_kernel,
        out_shape=jax.ShapeDtypeStruct((8, 128), F32),
        in_specs=[SMEM] + [ANY] * 6 + [VMEM] * 2,
        out_specs=VMEM,
        scratch_shapes=[
            pltpu.VMEM((PAIR, *pixels), BF),
            pltpu.VMEM(patch_w.shape, BF),
            pltpu.VMEM(w1.shape, BF),
            pltpu.VMEM(w2.shape, BF),
            pltpu.VMEM(w3.shape, BF),
            pltpu.VMEM(w4.shape, BF),
            *net_scratch(),
            pltpu.SemaphoreType.DMA((6,)),
        ],
        compiler_params=pltpu.CompilerParams(vmem_limit_bytes=40 << 20),
    )(left, views, patch_w, w1, w2, w3, w4, head, total)


def remainder(x, n, bound):
    for _ in range(bound - 1):
        x = jnp.where(x >= n, x - n, x)
    return x


def smooth_kernel(total, count, edges, bounds, labels, rim_out, rim_in, send_sem, recv_sem):
    s, c = lax.axis_index("span"), lax.axis_index("cnn")
    above, below = ((s + 1) % 8, c), ((s + 7) % 8, c)
    barrier = pltpu.get_barrier_semaphore()
    for other in (above, below):
        pl.semaphore_signal(barrier, inc=1, device_id=other, device_id_type=MESH)
    own_count = count[0, 0]
    row = lax.broadcasted_iota(I32, (8, 128), 0)
    alive = row < own_count
    smooth = jnp.where(alive, total[...], 0.0)
    border = 2 * RIM
    edge = edges[...]
    lookup = jnp.where(
        edge < border, edge, border + remainder(edge - border, own_count, SLOTS)
    )
    share = []
    for r in range(border + SLOTS):
        hits = (lookup == r).astype(F32)
        weight = hits[:, 0:1]
        for k in range(1, DEGREE):
            weight = weight + hits[:, k : k + 1]
        share.append(weight * (1.0 / DEGREE))
    exported_ids = [remainder(bounds[r], own_count, SLOTS) for r in range(RIM)]
    pl.semaphore_wait(barrier, 2)
    for step in range(ITERS):
        exported = jnp.zeros((8, 128), F32)
        for r in range(RIM):
            line = jnp.sum(jnp.where(row == exported_ids[r], smooth, 0.0), axis=0, keepdims=True)
            exported = jnp.where(row == r, line, exported)
        rim_out[step] = exported
        copies = []
        for side, other in enumerate((above, below)):
            copies.append(
                pltpu.make_async_remote_copy(
                    src_ref=rim_out.at[step], dst_ref=rim_in.at[step, side],
                    send_sem=send_sem.at[step, side], recv_sem=recv_sem.at[step, side],
                    device_id=other, device_id_type=MESH,
                )
            )
            copies[-1].start()
        mean = jnp.zeros((8, 128), F32)
        for r in range(SLOTS):
            mean = mean + share[border + r] * smooth[r : r + 1]
        for copy in copies:
            copy.wait()
        from_below = jnp.where(s > 0, rim_in[step, 0], 0.0)
        from_above = jnp.where(s < 7, rim_in[step, 1], 0.0)
        for r in range(RIM):
            mean = mean + share[r] * from_below[r : r + 1]
            mean = mean + share[RIM + r] * from_above[r : r + 1]
        smooth = jnp.where(alive, 0.5 * smooth + 0.5 * mean, 0.0)
    labels[...] = smooth[:, 0:CLASSES]


def smoothing(total, count, edges, bounds):
    dma = pltpu.SemaphoreType.DMA
    return pl.pallas_call(
        smooth_kernel,
        out_shape=jax.ShapeDtypeStruct((SLOTS, CLASSES), F32),
        in_specs=[VMEM, SMEM, VMEM, SMEM],
        out_specs=VMEM,
        scratch_shapes=[
            pltpu.VMEM((ITERS, 8, 128), F32),
            pltpu.VMEM((ITERS, 2, 8, 128), F32),
            dma((ITERS, 2)),
            dma((ITERS, 2)),
        ],
        compiler_params=pltpu.CompilerParams(collective_id=1, has_side_effects=True),
    )(total, count, edges, bounds)


def per_device(
    views, live_counts, skeleton_edges, boundary_rows,
    patch_weight, conv_first, conv_second, conv_third, conv_fourth, head_weight,
):
    weights = (
        patch_weight.reshape(64, 128),
        conv_first,
        conv_second,
        conv_third.reshape(1152, 256),
        conv_fourth.reshape(2304, 256),
        head_weight,
    )
    total, left = label(views, live_counts, *weights)
    total = rest(left, views, *weights, total)
    return smoothing(total, live_counts, skeleton_edges, boundary_rows)


def solution(mesh):
    placed = (
        P(("span", "cnn"), None, None, None, None),
        P("span", "cnn"),
        P(("span", "cnn"), None),
        P(("span", "cnn")),
        P(),
        P(),
        P(),
        P(),
        P(),
        P(),
    )
    return jax.shard_map(
        per_device, mesh=mesh, in_specs=placed, out_specs=P(("span", "cnn"), None), check_vma=False
    )
```

```python
import functools

import jax
import jax.numpy as jnp
from jax import lax
from jax.experimental import pallas as pl
from jax.experimental.pallas import tpu as pltpu
from jax.sharding import PartitionSpec as P

BF = jnp.bfloat16
F32 = jnp.float32
I32 = jnp.int32
MESH = pl.DeviceIdType.MESH
VMEM = pl.BlockSpec(memory_space=pltpu.VMEM)
SMEM = pl.BlockSpec(memory_space=pltpu.SMEM)
ANY = pl.BlockSpec(memory_space=pl.ANY)

VIEWS = 4
SLOTS = 8
RIM = 2
DEGREE = 4
ITERS = 2
CLASSES = 7
PAIR = 2
DIRS = 7
BACK = (0, 2, 1, 4, 3, 6, 5)
GOAL = 3
MOST = (3, 1)
ROUNDS = 4
ORDER = [(1, 0), (0, 0)] + [(half, d) for half in range(2) for d in range(1, DIRS)]
OWN = DIRS
OWN_LATE = OWN + SLOTS - 1
PLACES = OWN_LATE + SLOTS
FULL = (0, 256)


def dot(a, b):
    return jnp.dot(a, b, preferred_element_type=F32)


def rows_down(x):
    group = lax.broadcasted_iota(I32, x.shape, 0) % 16
    return jnp.where(group == 0, 0.0, pltpu.roll(x, 1, 0))


def rows_up(x):
    group = lax.broadcasted_iota(I32, x.shape, 0) % 16
    return jnp.where(group == 15, 0.0, pltpu.roll(x, x.shape[0] - 1, 0))


def prepare(patch_w, w1, w2, sel, wp, w1p, w2p, *maps):
    row = lax.broadcasted_iota(I32, (256, 256), 0)
    col = lax.broadcasted_iota(I32, (256, 256), 1)
    want = 16 * (row % 16) + 4 * ((row // 16) % 4) + row // 64
    sel[...] = jnp.where(col == want, 1.0, 0.0).astype(BF)
    row = lax.broadcasted_iota(I32, (512, 64), 0)
    col = lax.broadcasted_iota(I32, (512, 64), 1)
    dx, ch, dy = row // 128, (row // 32) % 4, row % 4
    spread = dot(jnp.where(col == dy * 16 + dx * 4 + ch, 1.0, 0.0).astype(BF), patch_w[...])
    r_of = (lax.broadcasted_iota(I32, (512, 128), 0) % 32) // 4
    for r in range(8):
        wp[:, r * 128 : (r + 1) * 128] = jnp.where(r_of == r, spread, 0.0).astype(BF)
    zero = jnp.zeros((128, 128), BF)
    for w, out in ((w1, w1p), (w2, w2p)):
        for dy in range(3):
            base = dy * 512
            for i, (even, odd) in enumerate(((1, 0), (2, 1), (0, None), (None, 2))):
                rows = pl.ds(base + i * 128, 128)
                out[rows, 0:128] = zero if even is None else w[dy, even]
                out[rows, 128:256] = zero if odd is None else w[dy, odd]
    for ref in maps:
        last = ref.shape[1] - 1
        for n in range(ref.shape[0]):
            ref[n, 0] = jnp.zeros(ref.shape[2:], BF)
            ref[n, last] = jnp.zeros(ref.shape[2:], BF)


def taps(parts, first, rows):
    pieces = []
    for dy in range(3):
        for ref, lanes in parts:
            piece = ref[pl.ds(first + dy, rows), :, lanes[0] : lanes[1]]
            pieces.append(piece.reshape(rows * piece.shape[1], piece.shape[2]))
    return jnp.concatenate(pieces, axis=1)


def tile_stage(load, sel, wp, xc, xs):
    pixels = jnp.concatenate([load(ch, 32 * b, 32) for b in range(4) for ch in range(4)], axis=0)
    moved = lax.dot_general(
        sel[...], pixels, (((1,), (1,)), ((), ())), preferred_element_type=F32
    ).astype(BF)
    tiles = jnp.concatenate(
        [
            jnp.concatenate(
                [moved[dx * 64 : (dx + 1) * 64, b * 128 : (b + 1) * 128] for dx in range(4)], axis=1
            )
            for b in range(4)
        ],
        axis=0,
    )
    for n in range(4):
        out = jnp.maximum(dot(tiles, wp[:, n * 256 : (n + 1) * 256]), 0.0)
        for half in range(2):
            lanes = out[:, half * 128 : (half + 1) * 128]
            for b in range(4):
                r = 1 + b * 8 + n * 2 + half
                q = [lanes[b * 64 + i * 16 : b * 64 + (i + 1) * 16] for i in range(4)]
                qb = [v.astype(BF) for v in q]
                xc[r, 0:16, 0:128] = qb[0]
                xc[r, 0:16, 128:256] = qb[1]
                xc[r, 16:32, 0:128] = qb[2]
                xc[r, 16:32, 128:256] = qb[3]
                xs[r, 0:16, 0:128] = rows_down(q[3]).astype(BF)
                xs[r, 0:16, 128:256] = qb[2]
                xs[r, 16:32, 0:128] = qb[1]
                xs[r, 16:32, 128:256] = rows_up(q[0]).astype(BF)


def first_stage(chunk, w1p, xc, xs, yc, ys):
    out = jnp.maximum(dot(taps(((xc, FULL), (xs, FULL)), chunk * 8, 8), w1p[...]), 0.0)
    pooled = (out[:, 0:128] + out[:, 128:256]).reshape(4, 2, 32, 128)
    pooled = (pooled[:, 0] + pooled[:, 1]) * 0.25
    even, odd = pooled[:, 0:16], pooled[:, 16:32]
    rows = pl.ds(1 + chunk * 4, 4)
    yc[rows, :, 0:128] = even.astype(BF)
    yc[rows, :, 128:256] = odd.astype(BF)
    ys[rows, :, 0:128] = rows_down(odd.reshape(64, 128)).astype(BF).reshape(4, 16, 128)
    ys[rows, :, 128:256] = rows_up(even.reshape(64, 128)).astype(BF).reshape(4, 16, 128)


def second_stage(w2p, yc, ys, tc, ts):
    out = jnp.maximum(dot(taps(((yc, FULL), (ys, FULL)), 0, 16), w2p[...]), 0.0)
    tc[1:17] = out.astype(BF).reshape(16, 16, 256)
    ts[1:17, :, 0:128] = rows_down(out[:, 128:256]).astype(BF).reshape(16, 16, 128)
    ts[1:17, :, 128:256] = rows_up(out[:, 0:128]).astype(BF).reshape(16, 16, 128)


def third_stage(w3, tc, ts, fe, fo, fm, fp):
    even = jnp.maximum(dot(taps(((ts, (0, 128)), (tc, FULL)), 0, 16), w3[...]), 0.0)
    odd = jnp.maximum(dot(taps(((tc, FULL), (ts, (128, 256))), 0, 16), w3[...]), 0.0)
    fe[1:17] = even.astype(BF).reshape(16, 16, 256)
    fo[1:17] = odd.astype(BF).reshape(16, 16, 256)
    fm[1:17] = rows_down(odd).astype(BF).reshape(16, 16, 256)
    fp[1:17] = rows_up(even).astype(BF).reshape(16, 16, 256)


def fourth_stage(w4, fe, fo, fm, fp):
    even = jnp.maximum(dot(taps(((fm, FULL), (fe, FULL), (fo, FULL)), 0, 16), w4[...]), 0.0)
    odd = jnp.maximum(dot(taps(((fe, FULL), (fo, FULL), (fp, FULL)), 0, 16), w4[...]), 0.0)
    return jnp.sum(even + odd, axis=0, keepdims=True) * (1.0 / 512)


def pair_feature(loads, w3, w4, sel, wp, w1p, w2p, *maps, between=lambda: None):
    own = [[m.at[v] for m in maps] for v in range(PAIR)]
    for v in range(PAIR):
        tile_stage(loads[v], sel, wp, *own[v][0:2])
        between()
    for chunk in range(4):
        for v in range(PAIR):
            first_stage(chunk, w1p, *own[v][0:4])
            between()
    for v in range(PAIR):
        second_stage(w2p, *own[v][2:6])
        between()
    for v in range(PAIR):
        third_stage(w3, *own[v][4:10])
        between()
    features = []
    for v in range(PAIR):
        features.append(fourth_stage(w4, *own[v][6:10]))
        between()
    return features[0] + features[1]


def net_scratch():
    shapes = [(256, 256), (512, 1024), (1536, 256), (1536, 256)]
    shapes += [(PAIR, 34, 32, 256)] * 2 + [(PAIR, 18, 16, 256)] * 8
    return [pltpu.VMEM(shape, BF) for shape in shapes]


def neighbours():
    s, c = lax.axis_index("span"), lax.axis_index("cnn")
    z, y = c // 4, c % 4
    return (
        (s + 1 - 2 * (s % 2), c),
        ((s + 2) % 8, c),
        ((s + 6) % 8, c),
        (s, (c + 4) % 16),
        (s, (c + 12) % 16),
        (s, z * 4 + (y + 1) % 4),
        (s, z * 4 + (y + 3) % 4),
    )


def seen(d, v):
    def ahead(n):
        return pltpu.roll(v, (128 - n) % 128, 1)

    g = lax.broadcasted_iota(I32, v.shape, 1)
    if d == 0:
        return jnp.where(g % 32 < 16, ahead(16), ahead(112))
    if d == 1:
        return ahead(32)
    if d == 2:
        return ahead(96)
    if d == 3:
        return jnp.where(g % 16 < 12, ahead(4), ahead(116))
    if d == 4:
        return jnp.where(g % 16 >= 4, ahead(124), ahead(12))
    if d == 5:
        return jnp.where(g % 4 < 3, ahead(1), ahead(125))
    return jnp.where(g % 4 >= 1, ahead(127), ahead(3))


def plan_steps(counts, plan):
    extra = counts - 1
    divisor = jnp.maximum(extra, 1)
    bit = []
    for d in range(DIRS):
        rest = jnp.full_like(counts, d)
        for _ in range(d):
            rest = jnp.where(rest >= divisor, rest - divisor, rest)
        bit.append(jnp.left_shift(jnp.ones_like(counts), 1 + rest))
    zero = jnp.zeros_like(counts)
    load = 2 * extra
    passed, taken, number = [zero, zero], [zero, zero], [zero, zero]
    near = zero
    for turn in range(ROUNDS):
        if turn:
            over = (load > GOAL).astype(I32)
            near = over
            for d in range(DIRS):
                near = near | seen(d, over)
        for half, d in ORDER:
            kind = half if d else 0
            open_here = (number[kind] < MOST[kind]) & (load < GOAL)
            there = seen(d, jnp.where(open_here, load + 16 * near, 64))
            wish = load > GOAL
            if turn:
                wish = wish | ((load >= GOAL - 1) & (near > 0) & (there < 16)) | (load - (there & 15) >= 2)
            push = wish & (there < 64) & ((passed[half] & bit[d]) == 0) & (extra > 0)
            gone = push.astype(I32)
            come = seen(BACK[d], gone)
            passed[half] = passed[half] | (gone * bit[d])
            taken[half] = taken[half] | (come << BACK[d])
            number[kind] = number[kind] + come
            load = load - gone + come
            yield
    plan.update(passed=passed, taken=taken, load=load)


def lowest(mask, places):
    place = jnp.int32(-1)
    for i in reversed(range(places)):
        place = jnp.where((mask >> i) & 1 == 1, jnp.int32(i), place)
    return place


def remote(src, dst, send_sem, recv_sem, device):
    return pltpu.make_async_remote_copy(
        src_ref=src, dst_ref=dst, send_sem=send_sem, recv_sem=recv_sem, device_id=device, device_id_type=MESH
    )


def remainder(x, n, bound):
    for _ in range(bound - 1):
        x = jnp.where(x >= n, x - n, x)
    return x


def smooth_steps(total, own_count, edges, bounds, rim_out, rim_in, send_sem, recv_sem):
    s, c = lax.axis_index("span"), lax.axis_index("cnn")
    row = lax.broadcasted_iota(I32, (8, 128), 0)
    lane = lax.broadcasted_iota(I32, (8, 128), 1)
    alive = row < own_count
    smooth = jnp.where(alive, total, 0.0)
    border = 2 * RIM
    weight = jnp.zeros((8, 128), F32)
    for k in range(DEGREE):
        edge = jnp.zeros((8, 128), I32)
        for place in range(SLOTS):
            edge = jnp.where(row == place, edges[k, place], edge)
        inner = border + remainder(edge - border, own_count, SLOTS)
        lookup = jnp.where(edge < border, edge, inner)
        weight = weight + jnp.where(lane == lookup, 1.0 / DEGREE, 0.0)
    share = [weight[:, r : r + 1] for r in range(border + SLOTS)]
    exported_ids = [remainder(bounds[r], own_count, SLOTS) for r in range(RIM)]
    for step in range(ITERS):
        exported = jnp.zeros((8, 128), F32)
        for r in range(RIM):
            line = jnp.sum(jnp.where(row == exported_ids[r], smooth, 0.0), axis=0, keepdims=True)
            exported = jnp.where(row == r, line, exported)
        rim_out[step] = exported
        copies = [
            remote(rim_out.at[step], rim_in.at[step, side], send_sem.at[step, side], recv_sem.at[step, side], other)
            for side, other in enumerate((((s + 1) % 8, c), ((s + 7) % 8, c)))
        ]
        for copy in copies:
            copy.start()
        mean = jnp.zeros((8, 128), F32)
        for r in range(SLOTS):
            mean = mean + share[border + r] * smooth[r : r + 1]
        for copy in copies:
            copy.wait()
        from_below = jnp.where(s > 0, rim_in[step, 0], 0.0)
        from_above = jnp.where(s < 7, rim_in[step, 1], 0.0)
        for r in range(RIM):
            mean = mean + share[r] * from_below[r : r + 1]
            mean = mean + share[RIM + r] * from_above[r : r + 1]
        smooth = jnp.where(alive, 0.5 * smooth + 0.5 * mean, 0.0)
    return smooth


def to_logits(units, head):
    logits = lax.dot_general(
        units, head[...], (((1,), (1,)), ((), ())),
        preferred_element_type=F32, precision=lax.Precision.HIGHEST,
    )
    return jnp.concatenate([logits * (1.0 / VIEWS), jnp.zeros((8, 128 - CLASSES), F32)], axis=1)


def label_kernel(
    views, count, edges, bounds, patch_w, w1_h, w2_h, w3_h, w4_h, head,
    labels, total_out, left_out,
    w1, w2, w3, w4, own0, own_a, own_b, own_c, own_d, early, late, send,
    mine, x_in, c_mine, c_in, back_out, back_in, rim_out, rim_in,
    sel, wp, w1p, w2p, m0, m1, m2, m3, m4, m5, m6, m7, m8, m9,
    own_sem, local_sem, weight_sem, view_send, view_recv,
    x_send, x_recv, c_send, c_recv, b_send, b_recv, r_send, r_recv,
):
    net = (sel, wp, w1p, w2p, m0, m1, m2, m3, m4, m5, m6, m7, m8, m9)
    s, c = lax.axis_index("span"), lax.axis_index("cnn")
    near = neighbours()
    along_x = [((s + o) % 8, c) for o in range(1, 8)]
    along_c = [(s, (c + o) % 16) for o in range(1, 16)]
    barrier = pltpu.get_barrier_semaphore()
    for other in along_x + along_c:
        pl.semaphore_signal(barrier, inc=1, device_id=other, device_id_type=MESH)

    own = ((own_a, own_b), (own_c, own_d))
    copies = [
        pltpu.make_async_copy(
            views.at[pl.ds(1, SLOTS - 1), half * PAIR + j], own[half][j], local_sem.at[half, j]
        )
        for half in range(2)
        for j in range(PAIR)
    ]
    first_copies = [
        pltpu.make_async_copy(src, dst, weight_sem.at[i])
        for i, (src, dst) in enumerate(((w1_h, w1), (w2_h, w2), (w3_h, w3), (w4_h, w4)))
    ]
    first_copies.append(pltpu.make_async_copy(views.at[0], own0, own_sem))
    for copy in copies[:1] + first_copies + copies[1:]:
        copy.start()

    own_count = count[0, 0]
    me = s * 16 + c
    lane = lax.broadcasted_iota(I32, (8, 128), 1)
    mine[...] = jnp.where(lane == me, own_count, 0)
    pl.semaphore_wait(barrier, len(along_x) + len(along_c))
    x_copies = [
        remote(mine, x_in.at[o], x_send.at[o], x_recv.at[o], along_x[o]) for o in range(7)
    ]
    for copy in x_copies:
        copy.start()

    divisor = jnp.maximum(own_count - 1, 1)
    slot = [jnp.int32(1) + lax.rem(jnp.int32(d), divisor) for d in range(DIRS)]
    early_copies, late_copies = [], []

    def pass_on(half, j, directions):
        for d in directions:
            for ch in range(4):
                send[half, j, d, ch] = own[half][j][jnp.clip(slot[d] - 1, 0, SLOTS - 2), ch]
            if half == 0:
                target = early.at[j, BACK[d]]
            elif d == 0:
                target = early.at[j, DIRS]
            else:
                target = late.at[j, BACK[d] - 1]
            copy = remote(
                send.at[half, j, d], target, view_send.at[half, j, d], view_recv.at[half, j, BACK[d]], near[d]
            )
            copy.start()
            (late_copies if half and d else early_copies).append(copy)

    copies[0].wait()
    pass_on(0, 0, range(DIRS))
    for copy in x_copies:
        copy.wait()
    counts = mine[...]
    for o in range(7):
        counts = counts + x_in[o]
    c_mine[...] = counts
    c_copies = [
        remote(c_mine, c_in.at[o], c_send.at[o], c_recv.at[o], along_c[o]) for o in range(15)
    ]
    for copy in c_copies:
        copy.start()
    for copy in copies[1:]:
        copy.wait()
    pass_on(0, 1, range(DIRS))
    pass_on(1, 0, range(1))
    pass_on(1, 1, range(1))
    pass_on(1, 0, range(1, DIRS))
    pass_on(1, 1, range(1, DIRS))
    for copy in first_copies:
        copy.wait()
    prepare(patch_w, w1, w2, *net)
    for copy in c_copies:
        copy.wait()
    for o in range(15):
        counts = counts + c_in[o]
    plan = {}
    steps = plan_steps(counts, plan)

    def go_on():
        for _ in range(2):
            next(steps, None)

    units = []
    for half in range(2):
        loads = [
            lambda ch, first, rows, v=half * PAIR + j: own0[v, ch, pl.ds(first, rows), :]
            for j in range(PAIR)
        ]
        units.append(pair_feature(loads, w3, w4, *net, between=go_on))
    for _ in steps:
        pass

    def here(v):
        return jnp.sum(jnp.where((lane == me)[0:1], v[0:1], 0))

    live = (jnp.left_shift(jnp.int32(1), own_count) - 1) & 254
    kept = [live & ~here(plan["passed"][half]) for half in range(2)]
    got = [here(plan["taken"][half]) for half in range(2)]
    mask = got[0] | ((got[1] & 1) << DIRS)
    mask = mask | ((kept[0] >> 1) << (OWN + 1)) | ((kept[1] >> 1) << (OWN_LATE + 1))
    picks = []
    for _ in range(GOAL):
        pick = lowest(mask, PLACES)
        picks.append(pick)
        last = jnp.where(pick >= 0, jnp.left_shift(jnp.int32(1), jnp.maximum(pick, 0)), 0)
        mask = mask & ~last
    third = picks[-1]
    late_dir = lowest(got[1] & ~1, DIRS)
    has_late = late_dir >= 0
    mask = mask | jnp.where(has_late, last, 0)
    picks[-1] = jnp.where(has_late, PLACES + late_dir, third)

    def at_place(place, j, ch, first, rows):
        pixels = [
            ref[jnp.clip(place - base, 0, most), ch, pl.ds(first, rows), :]
            for ref, base, most in (
                (early.at[j], 0, DIRS),
                (own[0][j], OWN + 1, SLOTS - 2),
                (own[1][j], OWN_LATE + 1, SLOTS - 2),
            )
        ]
        return jnp.where(
            place <= OWN, pixels[0], jnp.where(place <= OWN_LATE, pixels[1], pixels[2])
        )

    for copy in early_copies:
        copy.wait()
    for n in range(GOAL - 1):
        loads = [
            lambda ch, first, rows, j=j, n=n: at_place(picks[n], j, ch, first, rows)
            for j in range(PAIR)
        ]
        units.append(pair_feature(loads, w3, w4, *net))
    for copy in late_copies:
        copy.wait()
    place_late = jnp.clip(late_dir - 1, 0, DIRS - 2)
    loads = [
        lambda ch, first, rows, j=j: jnp.where(
            has_late,
            late[j, place_late, ch, pl.ds(first, rows), :],
            at_place(third, j, ch, first, rows),
        )
        for j in range(PAIR)
    ]
    units.append(pair_feature(loads, w3, w4, *net))

    logits = to_logits(jnp.concatenate(units + [jnp.zeros((8 - len(units), 256), F32)], axis=0), head)
    b_copies = []
    for d in range(DIRS):
        answer = jnp.zeros((8, 128), F32)
        for n, pick in enumerate(picks):
            ours = (pick == d) | (pick == PLACES + d)
            if d == 0:
                ours = ours | (pick == DIRS)
            answer = answer + jnp.where(ours, logits[2 + n : 3 + n], 0.0)
        back_out[d] = answer
        copy = remote(back_out.at[d], back_in.at[BACK[d]], b_send.at[d], b_recv.at[BACK[d]], near[d])
        copy.start()
        b_copies.append(copy)
    row = lax.broadcasted_iota(I32, (8, 128), 0)
    result = jnp.where(row == 0, logits[0:1] + logits[1:2], 0.0)
    for n, pick in enumerate(picks):
        for base in (OWN, OWN_LATE):
            is_own = (pick > base) & (pick < base + SLOTS) & (row == pick - base)
            result = result + jnp.where(is_own, logits[2 + n : 3 + n], 0.0)
    rest0 = (mask >> (OWN + 1)) & 127
    rest1 = (mask >> (OWN_LATE + 1)) & 127
    any_left = jnp.sum((plan["load"][0:1] > GOAL).astype(I32))
    left_out[...] = jnp.where(lane == 0, rest0 | (rest1 << 7), any_left)
    for copy in b_copies:
        copy.wait()
    for d in range(DIRS):
        result = result + jnp.where(row == slot[d], back_in[d], 0.0)
    total_out[...] = result
    smooth = smooth_steps(result, own_count, edges, bounds, rim_out, rim_in, r_send, r_recv)
    labels[...] = smooth[:, 0:CLASSES]


def label(views, count, edges, bounds, patch_w, w1, w2, w3, w4, head):
    dma = pltpu.SemaphoreType.DMA
    pixels = (4, 128, 256)
    tile = (8, 128)
    return pl.pallas_call(
        label_kernel,
        out_shape=(
            jax.ShapeDtypeStruct((SLOTS, CLASSES), F32),
            jax.ShapeDtypeStruct(tile, F32),
            jax.ShapeDtypeStruct(tile, I32),
        ),
        in_specs=[ANY, SMEM, SMEM, SMEM, VMEM, ANY, ANY, ANY, ANY, VMEM],
        out_specs=(VMEM, VMEM, VMEM),
        scratch_shapes=[
            *[pltpu.VMEM(w.shape, BF) for w in (w1, w2, w3, w4)],
            pltpu.VMEM((VIEWS, *pixels), BF),
            *[pltpu.VMEM((SLOTS - 1, *pixels), BF)] * (2 * PAIR),
            pltpu.VMEM((PAIR, DIRS + 1, *pixels), BF),
            pltpu.VMEM((PAIR, DIRS - 1, *pixels), BF),
            pltpu.VMEM((2, PAIR, DIRS, *pixels), BF),
            pltpu.VMEM(tile, I32),
            pltpu.VMEM((7, *tile), I32),
            pltpu.VMEM(tile, I32),
            pltpu.VMEM((15, *tile), I32),
            pltpu.VMEM((DIRS, *tile), F32),
            pltpu.VMEM((DIRS, *tile), F32),
            pltpu.VMEM((ITERS, *tile), F32),
            pltpu.VMEM((ITERS, 2, *tile), F32),
            *net_scratch(),
            dma(()), dma((2, PAIR)), dma((4,)),
            dma((2, PAIR, DIRS)), dma((2, PAIR, DIRS)),
            dma((7,)), dma((7,)), dma((15,)), dma((15,)), dma((DIRS,)), dma((DIRS,)),
            dma((ITERS, 2)), dma((ITERS, 2)),
        ],
        compiler_params=pltpu.CompilerParams(
            collective_id=0, has_side_effects=True, vmem_limit_bytes=58 << 20
        ),
    )(views, count, edges, bounds, patch_w, w1, w2, w3, w4, head)


def rest_kernel(
    left, views, patch_w, w1, w2, w3, w4, head, total,
    total_out, own, pw_v, w1_v, w2_v, w3_v, w4_v, *net_and_sems,
):
    net, sems = net_and_sems[:-1], net_and_sems[-1]
    mask = left[0, 0]
    total_out[...] = total[...]

    @pl.when(mask != 0)
    def _():
        moves = [
            pltpu.make_async_copy(a, b, sems.at[i])
            for i, (a, b) in enumerate(
                ((patch_w, pw_v), (w1, w1_v), (w2, w2_v), (w3, w3_v), (w4, w4_v))
            )
        ]
        for move in moves:
            move.start()
        for move in moves:
            move.wait()
        prepare(pw_v, w1_v, w2_v, *net)

        @pl.loop(0, 2 * (SLOTS - 1))
        def _(i):
            @pl.when((mask >> i) & 1 == 1)
            def _():
                slot, half = 1 + i % (SLOTS - 1), i // (SLOTS - 1)
                move = pltpu.make_async_copy(
                    views.at[slot, pl.ds(half * PAIR, PAIR)], own, sems.at[5]
                )
                move.start()
                move.wait()
                loads = [
                    lambda ch, first, rows, v=j: own[v, ch, pl.ds(first, rows), :]
                    for j in range(PAIR)
                ]
                unit = jnp.broadcast_to(pair_feature(loads, w3_v, w4_v, *net), (8, 256))
                logits = to_logits(unit, head)
                row = lax.broadcasted_iota(I32, (8, 128), 0)
                total_out[...] += jnp.where(row == slot, logits, 0.0)


def rest(left, views, patch_w, w1, w2, w3, w4, head, total):
    pixels = (4, 128, 256)
    return pl.pallas_call(
        rest_kernel,
        out_shape=jax.ShapeDtypeStruct((8, 128), F32),
        in_specs=[SMEM] + [ANY] * 6 + [VMEM] * 2,
        out_specs=VMEM,
        scratch_shapes=[
            pltpu.VMEM((PAIR, *pixels), BF),
            pltpu.VMEM(patch_w.shape, BF),
            pltpu.VMEM(w1.shape, BF),
            pltpu.VMEM(w2.shape, BF),
            pltpu.VMEM(w3.shape, BF),
            pltpu.VMEM(w4.shape, BF),
            *net_scratch(),
            pltpu.SemaphoreType.DMA((6,)),
        ],
        compiler_params=pltpu.CompilerParams(vmem_limit_bytes=58 << 20),
    )(left, views, patch_w, w1, w2, w3, w4, head, total)


def smooth_kernel(total, count, edges, bounds, labels, rim_out, rim_in, send_sem, recv_sem):
    s, c = lax.axis_index("span"), lax.axis_index("cnn")
    barrier = pltpu.get_barrier_semaphore()
    for other in (((s + 1) % 8, c), ((s + 7) % 8, c)):
        pl.semaphore_signal(barrier, inc=1, device_id=other, device_id_type=MESH)
    pl.semaphore_wait(barrier, 2)
    smooth = smooth_steps(
        total[...], count[0, 0], edges, bounds, rim_out, rim_in, send_sem, recv_sem
    )
    labels[...] = smooth[:, 0:CLASSES]


def smoothing(total, count, edges, bounds):
    dma = pltpu.SemaphoreType.DMA
    return pl.pallas_call(
        smooth_kernel,
        out_shape=jax.ShapeDtypeStruct((SLOTS, CLASSES), F32),
        in_specs=[VMEM, SMEM, SMEM, SMEM],
        out_specs=VMEM,
        scratch_shapes=[
            pltpu.VMEM((ITERS, 8, 128), F32),
            pltpu.VMEM((ITERS, 2, 8, 128), F32),
            dma((ITERS, 2)),
            dma((ITERS, 2)),
        ],
        compiler_params=pltpu.CompilerParams(collective_id=1, has_side_effects=True),
    )(total, count, edges, bounds)


def per_device(
    views, live_counts, skeleton_edges, boundary_rows,
    patch_weight, conv_first, conv_second, conv_third, conv_fourth, head_weight,
):
    weights = (
        patch_weight.reshape(64, 128),
        conv_first,
        conv_second,
        conv_third.reshape(1152, 256),
        conv_fourth.reshape(2304, 256),
        head_weight.T,
    )
    edges = skeleton_edges.T
    labels, total, left = label(views, live_counts, edges, boundary_rows, *weights)

    def with_rest():
        return smoothing(rest(left, views, *weights, total), live_counts, edges, boundary_rows)

    return lax.cond(left[0, 1] > 0, with_rest, lambda: labels)


def solution(mesh):
    placed = (
        P(("span", "cnn"), None, None, None, None),
        P("span", "cnn"),
        P(("span", "cnn"), None),
        P(("span", "cnn")),
        P(),
        P(),
        P(),
        P(),
        P(),
        P(),
    )
    return jax.shard_map(
        per_device, mesh=mesh, in_specs=placed, out_specs=P(("span", "cnn"), None), check_vma=False
    )
```

```python
import functools

import jax
import jax.numpy as jnp
from jax import lax
from jax.experimental import pallas as pl
from jax.experimental.pallas import tpu as pltpu
from jax.sharding import PartitionSpec as P

BF = jnp.bfloat16
F32 = jnp.float32
I32 = jnp.int32
MESH = pl.DeviceIdType.MESH
VMEM = pl.BlockSpec(memory_space=pltpu.VMEM)
SMEM = pl.BlockSpec(memory_space=pltpu.SMEM)
ANY = pl.BlockSpec(memory_space=pl.ANY)

VIEWS = 4
SLOTS = 8
RIM = 2
DEGREE = 4
ITERS = 2
CLASSES = 7
PAIR = 2
DIRS = 7
BACK = (0, 2, 1, 4, 3, 6, 5)
GOAL = 3
PLAN = (
    (False, (0,), 0),
    (False, (1,), 1),
    (True, (0,), 0),
    (True, (0, 1), 0),
    (True, (0, 1), 0),
)
OWN = DIRS
OWN_LATE = OWN + SLOTS - 1
PLACES = OWN_LATE + SLOTS
FULL = (0, 256)


def dot(a, b):
    return jnp.dot(a, b, preferred_element_type=F32)


def rows_down(x):
    group = lax.broadcasted_iota(I32, x.shape, 0) % 16
    return jnp.where(group == 0, 0.0, pltpu.roll(x, 1, 0))


def rows_up(x):
    group = lax.broadcasted_iota(I32, x.shape, 0) % 16
    return jnp.where(group == 15, 0.0, pltpu.roll(x, x.shape[0] - 1, 0))


def prepare(patch_w, w1, w2, sel, wp, w1p, w2p, *maps):
    row = lax.broadcasted_iota(I32, (256, 256), 0)
    col = lax.broadcasted_iota(I32, (256, 256), 1)
    want = 16 * (row % 16) + 4 * ((row // 16) % 4) + row // 64
    sel[...] = jnp.where(col == want, 1.0, 0.0).astype(BF)
    row = lax.broadcasted_iota(I32, (512, 64), 0)
    col = lax.broadcasted_iota(I32, (512, 64), 1)
    dx, ch, dy = row // 128, (row // 32) % 4, row % 4
    spread = dot(jnp.where(col == dy * 16 + dx * 4 + ch, 1.0, 0.0).astype(BF), patch_w[...])
    r_of = (lax.broadcasted_iota(I32, (512, 128), 0) % 32) // 4
    for r in range(8):
        wp[:, r * 128 : (r + 1) * 128] = jnp.where(r_of == r, spread, 0.0).astype(BF)
    zero = jnp.zeros((128, 128), BF)
    for w, out in ((w1, w1p), (w2, w2p)):
        for dy in range(3):
            base = dy * 512
            for i, (even, odd) in enumerate(((1, 0), (2, 1), (0, None), (None, 2))):
                rows = pl.ds(base + i * 128, 128)
                out[rows, 0:128] = zero if even is None else w[dy, even]
                out[rows, 128:256] = zero if odd is None else w[dy, odd]
    for ref in maps:
        last = ref.shape[1] - 1
        for n in range(ref.shape[0]):
            ref[n, 0] = jnp.zeros(ref.shape[2:], BF)
            ref[n, last] = jnp.zeros(ref.shape[2:], BF)


def taps(parts, first, rows):
    pieces = []
    for dy in range(3):
        for ref, lanes in parts:
            piece = ref[pl.ds(first + dy, rows), :, lanes[0] : lanes[1]]
            pieces.append(piece.reshape(rows * piece.shape[1], piece.shape[2]))
    return jnp.concatenate(pieces, axis=1)


def tile_stage(load, sel, wp, xc, xs):
    pixels = jnp.concatenate([load(ch, 32 * b, 32) for b in range(4) for ch in range(4)], axis=0)
    moved = lax.dot_general(
        sel[...], pixels, (((1,), (1,)), ((), ())), preferred_element_type=F32
    ).astype(BF)
    tiles = jnp.concatenate(
        [
            jnp.concatenate(
                [moved[dx * 64 : (dx + 1) * 64, b * 128 : (b + 1) * 128] for dx in range(4)], axis=1
            )
            for b in range(4)
        ],
        axis=0,
    )
    for n in range(4):
        out = jnp.maximum(dot(tiles, wp[:, n * 256 : (n + 1) * 256]), 0.0)
        for half in range(2):
            lanes = out[:, half * 128 : (half + 1) * 128]
            for b in range(4):
                r = 1 + b * 8 + n * 2 + half
                q = [lanes[b * 64 + i * 16 : b * 64 + (i + 1) * 16] for i in range(4)]
                qb = [v.astype(BF) for v in q]
                xc[r, 0:16, 0:128] = qb[0]
                xc[r, 0:16, 128:256] = qb[1]
                xc[r, 16:32, 0:128] = qb[2]
                xc[r, 16:32, 128:256] = qb[3]
                xs[r, 0:16, 0:128] = rows_down(q[3]).astype(BF)
                xs[r, 0:16, 128:256] = qb[2]
                xs[r, 16:32, 0:128] = qb[1]
                xs[r, 16:32, 128:256] = rows_up(q[0]).astype(BF)


def first_stage(chunk, w1p, xc, xs, yc, ys):
    out = jnp.maximum(dot(taps(((xc, FULL), (xs, FULL)), chunk * 8, 8), w1p[...]), 0.0)
    pooled = (out[:, 0:128] + out[:, 128:256]).reshape(4, 2, 32, 128)
    pooled = (pooled[:, 0] + pooled[:, 1]) * 0.25
    even, odd = pooled[:, 0:16], pooled[:, 16:32]
    rows = pl.ds(1 + chunk * 4, 4)
    yc[rows, :, 0:128] = even.astype(BF)
    yc[rows, :, 128:256] = odd.astype(BF)
    ys[rows, :, 0:128] = rows_down(odd.reshape(64, 128)).astype(BF).reshape(4, 16, 128)
    ys[rows, :, 128:256] = rows_up(even.reshape(64, 128)).astype(BF).reshape(4, 16, 128)


def second_stage(w2p, yc, ys, tc, ts):
    out = jnp.maximum(dot(taps(((yc, FULL), (ys, FULL)), 0, 16), w2p[...]), 0.0)
    tc[1:17] = out.astype(BF).reshape(16, 16, 256)
    ts[1:17, :, 0:128] = rows_down(out[:, 128:256]).astype(BF).reshape(16, 16, 128)
    ts[1:17, :, 128:256] = rows_up(out[:, 0:128]).astype(BF).reshape(16, 16, 128)


def third_stage(w3, tc, ts, fe, fo, fm, fp):
    even = jnp.maximum(dot(taps(((ts, (0, 128)), (tc, FULL)), 0, 16), w3[...]), 0.0)
    odd = jnp.maximum(dot(taps(((tc, FULL), (ts, (128, 256))), 0, 16), w3[...]), 0.0)
    fe[1:17] = even.astype(BF).reshape(16, 16, 256)
    fo[1:17] = odd.astype(BF).reshape(16, 16, 256)
    fm[1:17] = rows_down(odd).astype(BF).reshape(16, 16, 256)
    fp[1:17] = rows_up(even).astype(BF).reshape(16, 16, 256)


def fourth_stage(w4, fe, fo, fm, fp):
    even = jnp.maximum(dot(taps(((fm, FULL), (fe, FULL), (fo, FULL)), 0, 16), w4[...]), 0.0)
    odd = jnp.maximum(dot(taps(((fe, FULL), (fo, FULL), (fp, FULL)), 0, 16), w4[...]), 0.0)
    return jnp.sum(even + odd, axis=0, keepdims=True) * (1.0 / 512)


def pair_feature(loads, w3, w4, sel, wp, w1p, w2p, *maps, between=lambda: None):
    own = [[m.at[v] for m in maps] for v in range(PAIR)]
    for v in range(PAIR):
        tile_stage(loads[v], sel, wp, *own[v][0:2])
        between()
    for chunk in range(4):
        for v in range(PAIR):
            first_stage(chunk, w1p, *own[v][0:4])
            between()
    for v in range(PAIR):
        second_stage(w2p, *own[v][2:6])
        between()
    for v in range(PAIR):
        third_stage(w3, *own[v][4:10])
        between()
    features = []
    for v in range(PAIR):
        features.append(fourth_stage(w4, *own[v][6:10]))
        between()
    return features[0] + features[1]


def net_scratch():
    shapes = [(256, 256), (512, 1024), (1536, 256), (1536, 256)]
    shapes += [(PAIR, 34, 32, 256)] * 2 + [(PAIR, 18, 16, 256)] * 8
    return [pltpu.VMEM(shape, BF) for shape in shapes]


def neighbours():
    s, c = lax.axis_index("span"), lax.axis_index("cnn")
    z, y = c // 4, c % 4
    return (
        (s + 1 - 2 * (s % 2), c),
        ((s + 2) % 8, c),
        ((s + 6) % 8, c),
        (s, (c + 4) % 16),
        (s, (c + 12) % 16),
        (s, z * 4 + (y + 1) % 4),
        (s, z * 4 + (y + 3) % 4),
    )


def seen(d, v):
    def ahead(n):
        return pltpu.roll(v, (128 - n) % 128, 1)

    g = lax.broadcasted_iota(I32, v.shape, 1)
    if d == 0:
        return jnp.where(g % 32 < 16, ahead(16), ahead(112))
    if d == 1:
        return ahead(32)
    if d == 2:
        return ahead(96)
    if d == 3:
        return jnp.where(g % 16 < 12, ahead(4), ahead(116))
    if d == 4:
        return jnp.where(g % 16 >= 4, ahead(124), ahead(12))
    if d == 5:
        return jnp.where(g % 4 < 3, ahead(1), ahead(125))
    return jnp.where(g % 4 >= 1, ahead(127), ahead(3))


def plan_steps(counts, plan):
    extra = counts - 1
    divisor = jnp.maximum(extra, 1)
    bit = []
    for d in range(DIRS):
        rest = jnp.full_like(counts, d)
        for _ in range(d):
            rest = jnp.where(rest >= divisor, rest - divisor, rest)
        bit.append(jnp.left_shift(jnp.ones_like(counts), 1 + rest))
    zero = jnp.zeros_like(counts)
    load = 2 * extra
    passed, taken, late = [zero, zero], [zero, zero], zero
    near = zero
    for spread, halves, first in PLAN:
        if spread:
            over = (load > GOAL).astype(I32)
            near = over
            for d in range(DIRS):
                near = near | seen(d, over)
        for d in range(first, DIRS):
            there = seen(d, load + 16 * near + 32 * late)
            load_there, near_there, late_there = there & 15, there & 16, there & 32
            gone = [zero, zero]
            for half in halves if d else (1, 0):
                wish = load > GOAL
                if spread:
                    wish = wish | ((load >= GOAL - 1) & (near > 0) & (near_there == 0))
                    wish = wish | (load - load_there >= 2)
                push = wish & (load_there < GOAL) & ((passed[half] & bit[d]) == 0) & (extra > 0)
                if half and d:
                    push = push & (late_there == 0)
                gone[half] = push.astype(I32)
                passed[half] = passed[half] | (gone[half] * bit[d])
                load, load_there = load - gone[half], load_there + gone[half]
            come = seen(BACK[d], gone[0] + 2 * gone[1])
            came = [come & 1, come >> 1]
            for half in range(2):
                taken[half] = taken[half] | (came[half] << BACK[d])
            if d:
                late = late | came[1]
            load = load + came[0] + came[1]
            yield
    plan.update(passed=passed, taken=taken, load=load)


def lowest(mask, places):
    place = jnp.int32(-1)
    for i in reversed(range(places)):
        place = jnp.where((mask >> i) & 1 == 1, jnp.int32(i), place)
    return place


def remote(src, dst, send_sem, recv_sem, device):
    return pltpu.make_async_remote_copy(
        src_ref=src, dst_ref=dst, send_sem=send_sem, recv_sem=recv_sem, device_id=device, device_id_type=MESH
    )


def remainder(x, n, bound):
    for _ in range(bound - 1):
        x = jnp.where(x >= n, x - n, x)
    return x


def smooth_weights(edges, own_count, exported_below, exported_above):
    s = lax.axis_index("span")
    row = lax.broadcasted_iota(I32, (8, 128), 0)
    lane = lax.broadcasted_iota(I32, (8, 128), 1)
    rims = [jnp.where(s > 0, SLOTS + e, 127) for e in exported_below]
    rims += [jnp.where(s < 7, 2 * SLOTS + e, 127) for e in exported_above]
    weight = jnp.where(lane == row, 0.5, 0.0)
    for k in range(DEGREE):
        edge = jnp.zeros((8, 128), I32)
        for place in range(SLOTS):
            edge = jnp.where(row == place, edges[k, place], edge)
        target = remainder(edge - 2 * RIM, own_count, SLOTS)
        for r, rim in enumerate(rims):
            target = jnp.where(edge == r, rim, target)
        weight = weight + jnp.where(lane == target, 0.5 / DEGREE, 0.0)
    return jnp.where(row < own_count, weight, 0.0)


def spread_weights(weight, spread):
    for j in range(3 * SLOTS):
        spread[j] = jnp.broadcast_to(weight[:, j : j + 1], (8, 128))


def smooth_steps(smooth, spread, rim_out, rim_in, send_sem, recv_sem):
    s, c = lax.axis_index("span"), lax.axis_index("cnn")
    for step in range(ITERS):
        rim_out[step] = smooth
        copies = [
            remote(rim_out.at[step], rim_in.at[step, side], send_sem.at[step, side], recv_sem.at[step, side], other)
            for side, other in enumerate((((s + 1) % 8, c), ((s + 7) % 8, c)))
        ]
        for copy in copies:
            copy.start()
        sums = [jnp.zeros((8, 128), F32) for _ in range(4)]
        for r in range(SLOTS):
            sums[r % 4] = sums[r % 4] + spread[r] * rim_out[step, r : r + 1]
        for side, copy in enumerate(copies):
            copy.wait()
            for r in range(SLOTS):
                term = spread[SLOTS * (side + 1) + r] * rim_in[step, side, r : r + 1]
                sums[r % 4] = sums[r % 4] + term
        smooth = (sums[0] + sums[1]) + (sums[2] + sums[3])
    return smooth


def apply_weights(spread, own, below, above):
    sums = [jnp.zeros((8, 128), F32) for _ in range(4)]
    for i, rows in enumerate((own, below, above)):
        for r in range(SLOTS):
            sums[r % 4] = sums[r % 4] + spread[SLOTS * i + r] * rows[r : r + 1]
    return (sums[0] + sums[1]) + (sums[2] + sums[3])


def smooth_at_once(smooth, spread, rim_out, rim_in, send_sem, recv_sem):
    s, c = lax.axis_index("span"), lax.axis_index("cnn")
    rim_out[0] = smooth
    copies = [
        remote(rim_out.at[0], rim_in.at[i], send_sem.at[i], recv_sem.at[i], ((s + ahead) % 8, c))
        for i, ahead in enumerate((1, 7, 2, 6))
    ]
    for copy in copies:
        copy.start()
    for copy in copies:
        copy.wait()
    below, above, below2, above2 = [rim_in[i] for i in range(4)]
    own1 = apply_weights(spread.at[0], smooth, below, above)
    below1 = apply_weights(spread.at[1], below, below2, smooth)
    above1 = apply_weights(spread.at[2], above, smooth, above2)
    return apply_weights(spread.at[0], own1, below1, above1)


def to_logits(units, head):
    logits = lax.dot_general(
        units, head[...], (((1,), (1,)), ((), ())),
        preferred_element_type=F32, precision=lax.Precision.HIGHEST,
    )
    return jnp.concatenate([logits * (1.0 / VIEWS), jnp.zeros((8, 128 - CLASSES), F32)], axis=1)


def label_kernel(
    views, count, edges, bounds, patch_w, w1_h, w2_h, w3_h, w4_h, head,
    labels, more_out,
    w1, w2, w3, w4, own0, own_a, own_b, own_c, own_d, early, late, send,
    mine, x_in, c_mine, c_in, back_out, back_in, weight, weight_in, spread, rim_out, rim_in,
    sel, wp, w1p, w2p, m0, m1, m2, m3, m4, m5, m6, m7, m8, m9,
    own_sem, local_sem, weight_sem, view_send, view_recv,
    x_send, x_recv, c_send, c_recv, w_send, w_recv, b_send, b_recv, r_send, r_recv,
):
    net = (sel, wp, w1p, w2p, m0, m1, m2, m3, m4, m5, m6, m7, m8, m9)
    s, c = lax.axis_index("span"), lax.axis_index("cnn")
    near = neighbours()
    along_x = [((s + o) % 8, c) for o in range(1, 8)]
    along_c = [(s, (c + o) % 16) for o in range(1, 16)]
    barrier = pltpu.get_barrier_semaphore()
    for other in along_x + along_c:
        pl.semaphore_signal(barrier, inc=1, device_id=other, device_id_type=MESH)

    own = ((own_a, own_b), (own_c, own_d))
    copies = [
        pltpu.make_async_copy(
            views.at[pl.ds(1, SLOTS - 1), half * PAIR + j], own[half][j], local_sem.at[half, j]
        )
        for half in range(2)
        for j in range(PAIR)
    ]
    first_copies = [
        pltpu.make_async_copy(src, dst, weight_sem.at[i])
        for i, (src, dst) in enumerate(((w1_h, w1), (w2_h, w2), (w3_h, w3), (w4_h, w4)))
    ]
    first_copies.append(pltpu.make_async_copy(views.at[0], own0, own_sem))
    first_copies.insert(2, first_copies.pop())
    for copy in first_copies + copies:
        copy.start()

    own_count = count[0, 0]
    me = s * 16 + c
    lane = lax.broadcasted_iota(I32, (8, 128), 1)
    row = lax.broadcasted_iota(I32, (8, 128), 0)
    exported = [remainder(bounds[r], own_count, SLOTS) for r in range(RIM)]
    mine[...] = jnp.where(
        lane == me, jnp.where(row == 0, own_count, jnp.where(row == 1, exported[0], exported[1])), 0
    )
    x_copies = [
        remote(mine, x_in.at[o], x_send.at[o], x_recv.at[o], along_x[o]) for o in range(7)
    ]
    c_copies = [
        remote(c_mine, c_in.at[o], c_send.at[o], c_recv.at[o], along_c[o]) for o in range(15)
    ]

    divisor = jnp.maximum(own_count - 1, 1)
    slot = [jnp.int32(1) + lax.rem(jnp.int32(d), divisor) for d in range(DIRS)]
    early_copies, late_copies = [], []

    def fill(half, j, directions):
        for d in directions:
            for ch in range(4):
                send[half, j, d, ch] = own[half][j][jnp.clip(slot[d] - 1, 0, SLOTS - 2), ch]

    def pass_on(half, j, directions):
        for d in directions:
            if half == 0:
                target = early.at[j, BACK[d]]
            elif d == 0:
                target = early.at[j, DIRS]
            else:
                target = late.at[j, BACK[d] - 1]
            copy = remote(
                send.at[half, j, d], target, view_send.at[half, j, d], view_recv.at[half, j, BACK[d]], near[d]
            )
            copy.start()
            (late_copies if half and d else early_copies).append(copy)

    plan = {}

    def enter():
        pl.semaphore_wait(barrier, len(along_x) + len(along_c))
        for copy in x_copies:
            copy.start()

    def begin():
        copies[0].wait()
        fill(0, 0, range(DIRS))

    def counts_on():
        for copy in x_copies:
            copy.wait()
        counts = mine[...]
        for o in range(7):
            counts = counts + x_in[o]
        c_mine[...] = counts
        for copy in c_copies:
            copy.start()
        pass_on(0, 0, range(DIRS))

    def second_views():
        copies[1].wait()
        fill(0, 1, range(DIRS))
        pass_on(0, 1, range(DIRS))

    def second_halves():
        for j in range(PAIR):
            copies[PAIR + j].wait()
            fill(1, j, range(1))
            pass_on(1, j, range(1))

    def late_views(j):
        fill(1, j, range(1, DIRS))
        pass_on(1, j, range(1, DIRS))

    def weights_here():
        for copy in first_copies[3:]:
            copy.wait()

    w_copies = [
        remote(weight, weight_in.at[i], w_send.at[i], w_recv.at[i], along_x[ahead - 1])
        for i, ahead in enumerate((1, 7))
    ]

    def work():
        yield
        begin()
        counts_on()
        second_views()
        for _ in range(8):
            yield
        weights_here()
        second_halves()
        late_views(0)
        late_views(1)

    def planning():
        for copy in c_copies:
            copy.wait()
        counts = c_mine[...]
        for o in range(15):
            counts = counts + c_in[o]
        below = jnp.where(lane == lax.rem(me + 112, 128), counts, 0)
        above = jnp.where(lane == lax.rem(me + 16, 128), counts, 0)
        rims = [[jnp.sum(v[1 + r : 2 + r]) for r in range(RIM)] for v in (below, above)]
        weight[...] = smooth_weights(edges, own_count, *rims)
        for copy in w_copies:
            copy.start()
        for n, _ in enumerate(plan_steps(jnp.broadcast_to(counts[0:1], (8, 128)), plan)):
            if n % 3 == 2:
                yield

    def spreading():
        for i, tile in enumerate((weight, weight_in.at[0], weight_in.at[1])):
            spread_weights(tile[...], spread.at[i])
            yield

    enter()
    for copy in first_copies[:2]:
        copy.wait()
    prepare(patch_w, w1, w2, *net)
    first_copies[2].wait()

    units = []
    for half in range(2):
        loads = [
            lambda ch, first, rows, v=half * PAIR + j: own0[v, ch, pl.ds(first, rows), :]
            for j in range(PAIR)
        ]
        task = (work, planning)[half]()
        units.append(pair_feature(loads, w3, w4, *net, between=lambda task=task: next(task, None)))
        for _ in task:
            pass

    def here(v):
        return jnp.sum(jnp.where((lane == me)[0:1], v[0:1], 0))

    live = (jnp.left_shift(jnp.int32(1), own_count) - 1) & 254
    kept = [live & ~here(plan["passed"][half]) for half in range(2)]
    got = [here(plan["taken"][half]) for half in range(2)]
    mask = got[0] | ((got[1] & 1) << DIRS)
    mask = mask | ((kept[0] >> 1) << (OWN + 1)) | ((kept[1] >> 1) << (OWN_LATE + 1))
    picks = []
    for _ in range(GOAL):
        pick = lowest(mask, PLACES)
        picks.append(pick)
        last = jnp.where(pick >= 0, jnp.left_shift(jnp.int32(1), jnp.maximum(pick, 0)), 0)
        mask = mask & ~last
    third = picks[-1]
    late_dir = lowest(got[1] & ~1, DIRS)
    has_late = late_dir >= 0
    mask = mask | jnp.where(has_late, last, 0)
    picks[-1] = jnp.where(has_late, PLACES + late_dir, third)

    def at_place(place, j, ch, first, rows):
        pixels = [
            ref[jnp.clip(place - base, 0, most), ch, pl.ds(first, rows), :]
            for ref, base, most in (
                (early.at[j], 0, DIRS),
                (own[0][j], OWN + 1, SLOTS - 2),
                (own[1][j], OWN_LATE + 1, SLOTS - 2),
            )
        ]
        return jnp.where(
            place <= OWN, pixels[0], jnp.where(place <= OWN_LATE, pixels[1], pixels[2])
        )

    for copy in early_copies:
        copy.wait()
    for n in range(GOAL - 1):
        loads = [
            lambda ch, first, rows, j=j, n=n: at_place(picks[n], j, ch, first, rows)
            for j in range(PAIR)
        ]
        units.append(pair_feature(loads, w3, w4, *net))
    for copy in late_copies + w_copies:
        copy.wait()
    place_late = jnp.clip(late_dir - 1, 0, DIRS - 2)
    loads = [
        lambda ch, first, rows, j=j: jnp.where(
            has_late,
            late[j, place_late, ch, pl.ds(first, rows), :],
            at_place(third, j, ch, first, rows),
        )
        for j in range(PAIR)
    ]
    task = spreading()
    units.append(pair_feature(loads, w3, w4, *net, between=lambda: next(task, None)))

    logits = to_logits(jnp.concatenate(units + [jnp.zeros((8 - len(units), 256), F32)], axis=0), head)
    b_copies = []
    for d in range(DIRS):
        answer = jnp.zeros((8, 128), F32)
        for n, pick in enumerate(picks):
            ours = (pick == d) | (pick == PLACES + d)
            if d == 0:
                ours = ours | (pick == DIRS)
            answer = answer + jnp.where(ours, logits[2 + n : 3 + n], 0.0)
        back_out[d] = answer
        copy = remote(back_out.at[d], back_in.at[BACK[d]], b_send.at[d], b_recv.at[BACK[d]], near[d])
        copy.start()
        b_copies.append(copy)
    result = jnp.where(row == 0, logits[0:1] + logits[1:2], 0.0)
    for n, pick in enumerate(picks):
        for base in (OWN, OWN_LATE):
            is_own = (pick > base) & (pick < base + SLOTS) & (row == pick - base)
            result = result + jnp.where(is_own, logits[2 + n : 3 + n], 0.0)
    rest0 = (mask >> (OWN + 1)) & 127
    rest1 = (mask >> (OWN_LATE + 1)) & 127
    any_left = jnp.sum((plan["load"][0:1] > GOAL).astype(I32))
    more_out[2] = jnp.where(lane == 0, rest0 | (rest1 << 7), any_left).astype(F32)
    more_out[1] = weight[...]
    for copy in b_copies:
        copy.wait()
    for d in range(DIRS):
        result = result + jnp.where(row == slot[d], back_in[d], 0.0)
    result = jnp.where(row < own_count, result, 0.0)
    more_out[0] = result
    smooth = smooth_at_once(result, spread, rim_out, rim_in, r_send, r_recv)
    labels[...] = smooth[:, 0:CLASSES]


def label(views, count, edges, bounds, patch_w, w1, w2, w3, w4, head):
    dma = pltpu.SemaphoreType.DMA
    pixels = (4, 128, 256)
    tile = (8, 128)
    return pl.pallas_call(
        label_kernel,
        out_shape=(
            jax.ShapeDtypeStruct((SLOTS, CLASSES), F32),
            jax.ShapeDtypeStruct((3, *tile), F32),
        ),
        in_specs=[ANY, SMEM, SMEM, SMEM, VMEM, ANY, ANY, ANY, ANY, VMEM],
        out_specs=(VMEM, VMEM),
        scratch_shapes=[
            *[pltpu.VMEM(w.shape, BF) for w in (w1, w2, w3, w4)],
            pltpu.VMEM((VIEWS, *pixels), BF),
            *[pltpu.VMEM((SLOTS - 1, *pixels), BF)] * (2 * PAIR),
            pltpu.VMEM((PAIR, DIRS + 1, *pixels), BF),
            pltpu.VMEM((PAIR, DIRS - 1, *pixels), BF),
            pltpu.VMEM((2, PAIR, DIRS, *pixels), BF),
            pltpu.VMEM(tile, I32),
            pltpu.VMEM((7, *tile), I32),
            pltpu.VMEM(tile, I32),
            pltpu.VMEM((15, *tile), I32),
            pltpu.VMEM((DIRS, *tile), F32),
            pltpu.VMEM((DIRS, *tile), F32),
            pltpu.VMEM(tile, F32),
            pltpu.VMEM((2, *tile), F32),
            pltpu.VMEM((3, 3 * SLOTS, *tile), F32),
            pltpu.VMEM((1, *tile), F32),
            pltpu.VMEM((4, *tile), F32),
            *net_scratch(),
            dma(()), dma((2, PAIR)), dma((4,)),
            dma((2, PAIR, DIRS)), dma((2, PAIR, DIRS)),
            dma((7,)), dma((7,)), dma((15,)), dma((15,)), dma((2,)), dma((2,)),
            dma((DIRS,)), dma((DIRS,)), dma((4,)), dma((4,)),
        ],
        compiler_params=pltpu.CompilerParams(
            collective_id=0, has_side_effects=True, vmem_limit_bytes=58 << 20
        ),
    )(views, count, edges, bounds, patch_w, w1, w2, w3, w4, head)


def rest_kernel(
    left, views, patch_w, w1, w2, w3, w4, head, total,
    total_out, own, pw_v, w1_v, w2_v, w3_v, w4_v, *net_and_sems,
):
    net, sems = net_and_sems[:-1], net_and_sems[-1]
    mask = left[0, 0].astype(I32)
    total_out[...] = total[...]

    @pl.when(mask != 0)
    def _():
        moves = [
            pltpu.make_async_copy(a, b, sems.at[i])
            for i, (a, b) in enumerate(
                ((patch_w, pw_v), (w1, w1_v), (w2, w2_v), (w3, w3_v), (w4, w4_v))
            )
        ]
        for move in moves:
            move.start()
        for move in moves:
            move.wait()
        prepare(pw_v, w1_v, w2_v, *net)

        @pl.loop(0, 2 * (SLOTS - 1))
        def _(i):
            @pl.when((mask >> i) & 1 == 1)
            def _():
                slot, half = 1 + i % (SLOTS - 1), i // (SLOTS - 1)
                move = pltpu.make_async_copy(
                    views.at[slot, pl.ds(half * PAIR, PAIR)], own, sems.at[5]
                )
                move.start()
                move.wait()
                loads = [
                    lambda ch, first, rows, v=j: own[v, ch, pl.ds(first, rows), :]
                    for j in range(PAIR)
                ]
                unit = jnp.broadcast_to(pair_feature(loads, w3_v, w4_v, *net), (8, 256))
                logits = to_logits(unit, head)
                row = lax.broadcasted_iota(I32, (8, 128), 0)
                total_out[...] += jnp.where(row == slot, logits, 0.0)


def rest(left, views, patch_w, w1, w2, w3, w4, head, total):
    pixels = (4, 128, 256)
    return pl.pallas_call(
        rest_kernel,
        out_shape=jax.ShapeDtypeStruct((8, 128), F32),
        in_specs=[SMEM] + [ANY] * 6 + [VMEM] * 2,
        out_specs=VMEM,
        scratch_shapes=[
            pltpu.VMEM((PAIR, *pixels), BF),
            pltpu.VMEM(patch_w.shape, BF),
            pltpu.VMEM(w1.shape, BF),
            pltpu.VMEM(w2.shape, BF),
            pltpu.VMEM(w3.shape, BF),
            pltpu.VMEM(w4.shape, BF),
            *net_scratch(),
            pltpu.SemaphoreType.DMA((6,)),
        ],
        compiler_params=pltpu.CompilerParams(vmem_limit_bytes=58 << 20),
    )(left, views, patch_w, w1, w2, w3, w4, head, total)


def smooth_kernel(total, weight, labels, spread, rim_out, rim_in, send_sem, recv_sem):
    s, c = lax.axis_index("span"), lax.axis_index("cnn")
    barrier = pltpu.get_barrier_semaphore()
    for other in (((s + 1) % 8, c), ((s + 7) % 8, c)):
        pl.semaphore_signal(barrier, inc=1, device_id=other, device_id_type=MESH)
    spread_weights(weight[...], spread)
    pl.semaphore_wait(barrier, 2)
    smooth = smooth_steps(total[...], spread, rim_out, rim_in, send_sem, recv_sem)
    labels[...] = smooth[:, 0:CLASSES]


def smoothing(total, weight):
    dma = pltpu.SemaphoreType.DMA
    return pl.pallas_call(
        smooth_kernel,
        out_shape=jax.ShapeDtypeStruct((SLOTS, CLASSES), F32),
        in_specs=[VMEM, VMEM],
        out_specs=VMEM,
        scratch_shapes=[
            pltpu.VMEM((3 * SLOTS, 8, 128), F32),
            pltpu.VMEM((ITERS, 8, 128), F32),
            pltpu.VMEM((ITERS, 2, 8, 128), F32),
            dma((ITERS, 2)),
            dma((ITERS, 2)),
        ],
        compiler_params=pltpu.CompilerParams(collective_id=1, has_side_effects=True),
    )(total, weight)


def per_device(
    views, live_counts, skeleton_edges, boundary_rows,
    patch_weight, conv_first, conv_second, conv_third, conv_fourth, head_weight,
):
    weights = (
        patch_weight.reshape(64, 128),
        conv_first,
        conv_second,
        conv_third.reshape(1152, 256),
        conv_fourth.reshape(2304, 256),
        head_weight.T,
    )
    labels, more = label(views, live_counts, skeleton_edges.T, boundary_rows, *weights)

    def with_rest():
        return smoothing(rest(more[2], views, *weights, more[0]), more[1])

    return lax.cond(more[2, 0, 1] > 0, with_rest, lambda: labels)


def solution(mesh):
    placed = (
        P(("span", "cnn"), None, None, None, None),
        P("span", "cnn"),
        P(("span", "cnn"), None),
        P(("span", "cnn")),
        P(),
        P(),
        P(),
        P(),
        P(),
        P(),
    )
    return jax.shard_map(
        per_device, mesh=mesh, in_specs=placed, out_specs=P(("span", "cnn"), None), check_vma=False
    )
```

```python
import functools

import jax
import jax.numpy as jnp
from jax import lax
from jax.experimental import pallas as pl
from jax.experimental.pallas import tpu as pltpu
from jax.sharding import PartitionSpec as P

BF = jnp.bfloat16
F32 = jnp.float32
I32 = jnp.int32
MESH = pl.DeviceIdType.MESH
VMEM = pl.BlockSpec(memory_space=pltpu.VMEM)
SMEM = pl.BlockSpec(memory_space=pltpu.SMEM)
ANY = pl.BlockSpec(memory_space=pl.ANY)

VIEWS = 4
SLOTS = 8
RIM = 2
DEGREE = 4
ITERS = 2
CLASSES = 7
PAIR = 2
DIRS = 7
BACK = (0, 2, 1, 4, 3, 6, 5)
GOAL = 3
PLAN = (
    (False, (0,), 0),
    (False, (1,), 1),
    (True, (0,), 0),
    (True, (0, 1), 0),
    (True, (0, 1), 0),
)
OWN = DIRS
OWN_LATE = OWN + SLOTS - 1
PLACES = OWN_LATE + SLOTS
FULL = (0, 256)


def dot(a, b):
    return jnp.dot(a, b, preferred_element_type=F32)


def rows_down(x):
    group = lax.broadcasted_iota(I32, x.shape, 0) % 16
    return jnp.where(group == 0, 0.0, pltpu.roll(x, 1, 0))


def rows_up(x):
    group = lax.broadcasted_iota(I32, x.shape, 0) % 16
    return jnp.where(group == 15, 0.0, pltpu.roll(x, x.shape[0] - 1, 0))


def prepare(patch_w, w1, w2, sel, wp, w1p, w2p, *maps):
    row = lax.broadcasted_iota(I32, (256, 256), 0)
    col = lax.broadcasted_iota(I32, (256, 256), 1)
    turn = row // 64
    want = 16 * (row % 16) + 4 * ((row // 16) % 4) + 2 * (turn % 2) + turn // 2
    sel[...] = jnp.where(col == want, 1.0, 0.0).astype(BF)
    row = lax.broadcasted_iota(I32, (512, 64), 0)
    col = lax.broadcasted_iota(I32, (512, 64), 1)
    dx, ch, dy = (row // 64) % 4, (row // 16) % 4, row % 4
    dx = jnp.where(row < 256, dx, dx + 1 - 2 * (dx % 2))
    spread = dot(jnp.where(col == dy * 16 + dx * 4 + ch, 1.0, 0.0).astype(BF), patch_w[...])
    r_of = (lax.broadcasted_iota(I32, (512, 128), 0) % 16) // 4
    for r in range(4):
        wp[:, r * 128:(r + 1) * 128] = jnp.where(r_of == r, spread, 0.0).astype(BF)
    zero = jnp.zeros((128, 128), BF)
    for w, out in ((w1, w1p), (w2, w2p)):
        for dy in range(3):
            for i, (even, odd) in enumerate(((1, 0), (2, 1))):
                rows = pl.ds(dy * 256 + i * 128, 128)
                out[rows, 0:128] = w[dy, even]
                out[rows, 128:256] = w[dy, odd]
        for side, dx in enumerate((0, 2)):
            for i in range(4):
                rows = pl.ds(768 + side * 512 + i * 128, 128)
                out[rows, 0:128] = w[i, dx] if i < 3 else zero
                out[rows, 128:256] = w[i - 1, dx] if i else zero
    for ref in maps:
        last = ref.shape[1] - 1
        for n in range(ref.shape[0]):
            ref[n, 0] = jnp.zeros(ref.shape[2:], BF)
            ref[n, last] = jnp.zeros(ref.shape[2:], BF)


def taps(parts, first, rows):
    pieces = []
    for dy in range(3):
        for ref, lanes in parts:
            piece = ref[pl.ds(first + dy, rows), :, lanes[0] : lanes[1]]
            pieces.append(piece.reshape(rows * piece.shape[1], piece.shape[2]))
    return jnp.concatenate(pieces, axis=1)


def tile_stage(load, sel, wp, xc, xs):
    moved = []
    for odd in range(2):
        pixels = jnp.concatenate(
            [load(ch, 32 * b + 16 * (g ^ odd), 16) for b in range(4) for g in range(2) for ch in range(4)], axis=0)
        moved.append(lax.dot_general(sel[odd * 128:(odd + 1) * 128], pixels, (((1,), (1,)), ((), ())),
                                     preferred_element_type=F32))
    low = lax.broadcasted_iota(I32, (64, 128), 1) < 64
    tiles = [[], []]
    for b in range(4):
        lanes = slice(b * 128, (b + 1) * 128)
        even = [moved[0][i * 64:(i + 1) * 64, lanes] for i in range(2)]
        odd = [moved[1][i * 64:(i + 1) * 64, lanes] for i in range(2)]
        tiles[0].append(jnp.concatenate([jnp.where(low, even[i], odd[i]).astype(BF) for i in range(2)], axis=1))
        tiles[1].append(jnp.concatenate([jnp.where(low, odd[i], even[i]).astype(BF) for i in range(2)], axis=1))
    tiles = [jnp.concatenate(t, axis=0) for t in tiles]
    for n in range(4):
        g = n // 2
        out = jnp.maximum(dot(tiles[g], wp[g * 256:(g + 1) * 256, (n % 2) * 256:(n % 2 + 1) * 256]), 0.0)
        for half in range(2):
            lanes = out[:, half * 128:(half + 1) * 128]
            for b in range(4):
                r = 1 + b * 8 + n * 2 + half
                q = [lanes[b * 64 + i * 16:b * 64 + (i + 1) * 16] for i in range(4)]
                qb = [v.astype(BF) for v in q]
                xc[r, 0:16, 0:128] = qb[0]
                xc[r, 0:16, 128:256] = qb[1]
                xc[r, 16:32, 0:128] = qb[2]
                xc[r, 16:32, 128:256] = qb[3]
                xs[r, 0:16, 0:128] = rows_down(q[3]).astype(BF)
                xs[r, 0:16, 128:256] = qb[2]
                xs[r, 16:32, 0:128] = qb[1]
                xs[r, 16:32, 128:256] = rows_up(q[0]).astype(BF)


def pair_conv(center, sides, wp, first, rows):
    c = center.shape[1]
    mid = dot(taps(((center, (0, 256)),), first, rows), wp[0:768])
    mid = mid.reshape(rows // 2, 2, c, 256)
    halves = []
    for side in range(2):
        pieces = []
        for i in range(4):
            lanes = [sides[first + 2 * p + i, :, side * 128:(side + 1) * 128] for p in range(rows // 2)]
            pieces.append(jnp.concatenate(lanes, axis=0))
        out = dot(jnp.concatenate(pieces, axis=1), wp[768 + side * 512:1280 + side * 512])
        halves.append(out.reshape(rows // 2, c, 256))
    result = []
    for r in range(2):
        lanes = slice(r * 128, (r + 1) * 128)
        result.append([jnp.maximum(mid[:, r, :, 0:128] + halves[0][:, :, lanes], 0.0),
                       jnp.maximum(mid[:, r, :, 128:256] + halves[1][:, :, lanes], 0.0)])
    return result


def first_stage(chunk, w1p, xc, xs, yc, ys):
    out = pair_conv(xc, xs, w1p, chunk * 8, 8)
    pooled = ((out[0][0] + out[0][1]) + (out[1][0] + out[1][1])) * 0.25
    even, odd = pooled[:, 0:16], pooled[:, 16:32]
    rows = pl.ds(1 + chunk * 4, 4)
    yc[rows, :, 0:128] = even.astype(BF)
    yc[rows, :, 128:256] = odd.astype(BF)
    ys[rows, :, 0:128] = rows_down(odd.reshape(64, 128)).astype(BF).reshape(4, 16, 128)
    ys[rows, :, 128:256] = rows_up(even.reshape(64, 128)).astype(BF).reshape(4, 16, 128)


def second_stage(w2p, yc, ys, tc, ts):
    out = pair_conv(yc, ys, w2p, 0, 16)
    for r in range(2):
        even, odd = out[r]
        down = rows_down(odd.reshape(128, 128)).astype(BF).reshape(8, 16, 128)
        up = rows_up(even.reshape(128, 128)).astype(BF).reshape(8, 16, 128)
        for p in range(8):
            at = 1 + 2 * p + r
            tc[at, :, 0:128] = even[p].astype(BF)
            tc[at, :, 128:256] = odd[p].astype(BF)
            ts[at, :, 0:128] = down[p]
            ts[at, :, 128:256] = up[p]


def third_stage(w3, tc, ts, fe, fo, fm, fp):
    even = jnp.maximum(dot(taps(((ts, (0, 128)), (tc, FULL)), 0, 16), w3[...]), 0.0)
    odd = jnp.maximum(dot(taps(((tc, FULL), (ts, (128, 256))), 0, 16), w3[...]), 0.0)
    fe[1:17] = even.astype(BF).reshape(16, 16, 256)
    fo[1:17] = odd.astype(BF).reshape(16, 16, 256)
    fm[1:17] = rows_down(odd).astype(BF).reshape(16, 16, 256)
    fp[1:17] = rows_up(even).astype(BF).reshape(16, 16, 256)


def fourth_stage(w4, fe, fo, fm, fp):
    even = jnp.maximum(dot(taps(((fm, FULL), (fe, FULL), (fo, FULL)), 0, 16), w4[...]), 0.0)
    odd = jnp.maximum(dot(taps(((fe, FULL), (fo, FULL), (fp, FULL)), 0, 16), w4[...]), 0.0)
    return jnp.sum(even + odd, axis=0, keepdims=True) * (1.0 / 512)


def pair_feature(loads, w3, w4, sel, wp, w1p, w2p, *maps, between=lambda: None):
    own = [[m.at[v] for m in maps] for v in range(PAIR)]
    for v in range(PAIR):
        tile_stage(loads[v], sel, wp, *own[v][0:2])
        between()
    for chunk in range(4):
        for v in range(PAIR):
            first_stage(chunk, w1p, *own[v][0:4])
            between()
    for v in range(PAIR):
        second_stage(w2p, *own[v][2:6])
        between()
    for v in range(PAIR):
        third_stage(w3, *own[v][4:10])
        between()
    features = []
    for v in range(PAIR):
        features.append(fourth_stage(w4, *own[v][6:10]))
        between()
    return features[0] + features[1]


def net_scratch():
    shapes = [(256, 256), (512, 512), (1792, 256), (1792, 256)]
    shapes += [(PAIR, 34, 32, 256)] * 2 + [(PAIR, 18, 16, 256)] * 8
    return [pltpu.VMEM(shape, BF) for shape in shapes]


def neighbours():
    s, c = lax.axis_index("span"), lax.axis_index("cnn")
    z, y = c // 4, c % 4
    return (
        (s + 1 - 2 * (s % 2), c),
        ((s + 2) % 8, c),
        ((s + 6) % 8, c),
        (s, (c + 4) % 16),
        (s, (c + 12) % 16),
        (s, z * 4 + (y + 1) % 4),
        (s, z * 4 + (y + 3) % 4),
    )


def seen(d, v):
    def ahead(n):
        return pltpu.roll(v, (128 - n) % 128, 1)

    g = lax.broadcasted_iota(I32, v.shape, 1)
    if d == 0:
        return jnp.where(g % 32 < 16, ahead(16), ahead(112))
    if d == 1:
        return ahead(32)
    if d == 2:
        return ahead(96)
    if d == 3:
        return jnp.where(g % 16 < 12, ahead(4), ahead(116))
    if d == 4:
        return jnp.where(g % 16 >= 4, ahead(124), ahead(12))
    if d == 5:
        return jnp.where(g % 4 < 3, ahead(1), ahead(125))
    return jnp.where(g % 4 >= 1, ahead(127), ahead(3))


def plan_steps(counts, plan):
    extra = counts - 1
    divisor = jnp.maximum(extra, 1)
    bit = []
    for d in range(DIRS):
        rest = jnp.full_like(counts, d)
        for _ in range(d):
            rest = jnp.where(rest >= divisor, rest - divisor, rest)
        bit.append(jnp.left_shift(jnp.ones_like(counts), 1 + rest))
    zero = jnp.zeros_like(counts)
    load = 2 * extra
    passed, taken, late = [zero, zero], [zero, zero], zero
    near = zero
    for spread, halves, first in PLAN:
        if spread:
            over = (load > GOAL).astype(I32)
            near = over
            for d in range(DIRS):
                near = near | seen(d, over)
        for d in range(first, DIRS):
            there = seen(d, load + 16 * near + 32 * late)
            load_there, near_there, late_there = there & 15, there & 16, there & 32
            gone = [zero, zero]
            for half in halves if d else (1, 0):
                wish = load > GOAL
                if spread:
                    wish = wish | ((load >= GOAL - 1) & (near > 0) & (near_there == 0))
                    wish = wish | (load - load_there >= 2)
                push = wish & (load_there < GOAL) & ((passed[half] & bit[d]) == 0) & (extra > 0)
                if half and d:
                    push = push & (late_there == 0)
                gone[half] = push.astype(I32)
                passed[half] = passed[half] | (gone[half] * bit[d])
                load, load_there = load - gone[half], load_there + gone[half]
            come = seen(BACK[d], gone[0] + 2 * gone[1])
            came = [come & 1, come >> 1]
            for half in range(2):
                taken[half] = taken[half] | (came[half] << BACK[d])
            if d:
                late = late | came[1]
            load = load + came[0] + came[1]
            yield
    plan.update(passed=passed, taken=taken, load=load)


def lowest(mask, places):
    place = jnp.int32(-1)
    for i in reversed(range(places)):
        place = jnp.where((mask >> i) & 1 == 1, jnp.int32(i), place)
    return place


def remote(src, dst, send_sem, recv_sem, device):
    return pltpu.make_async_remote_copy(
        src_ref=src, dst_ref=dst, send_sem=send_sem, recv_sem=recv_sem, device_id=device, device_id_type=MESH
    )


def remainder(x, n, bound):
    for _ in range(bound - 1):
        x = jnp.where(x >= n, x - n, x)
    return x


def smooth_weights(edges, own_count, exported_below, exported_above):
    s = lax.axis_index("span")
    row = lax.broadcasted_iota(I32, (8, 128), 0)
    lane = lax.broadcasted_iota(I32, (8, 128), 1)
    rims = [jnp.where(s > 0, SLOTS + e, 127) for e in exported_below]
    rims += [jnp.where(s < 7, 2 * SLOTS + e, 127) for e in exported_above]
    weight = jnp.where(lane == row, 0.5, 0.0)
    for k in range(DEGREE):
        edge = jnp.zeros((8, 128), I32)
        for place in range(SLOTS):
            edge = jnp.where(row == place, edges[k, place], edge)
        target = remainder(edge - 2 * RIM, own_count, SLOTS)
        for r, rim in enumerate(rims):
            target = jnp.where(edge == r, rim, target)
        weight = weight + jnp.where(lane == target, 0.5 / DEGREE, 0.0)
    return jnp.where(row < own_count, weight, 0.0)


def spread_weights(weight, spread):
    for j in range(3 * SLOTS):
        spread[j] = jnp.broadcast_to(weight[:, j : j + 1], (8, 128))


def smooth_steps(smooth, spread, rim_out, rim_in, send_sem, recv_sem):
    s, c = lax.axis_index("span"), lax.axis_index("cnn")
    for step in range(ITERS):
        rim_out[step] = smooth
        copies = [
            remote(rim_out.at[step], rim_in.at[step, side], send_sem.at[step, side], recv_sem.at[step, side], other)
            for side, other in enumerate((((s + 1) % 8, c), ((s + 7) % 8, c)))
        ]
        for copy in copies:
            copy.start()
        sums = [jnp.zeros((8, 128), F32) for _ in range(4)]
        for r in range(SLOTS):
            sums[r % 4] = sums[r % 4] + spread[r] * rim_out[step, r : r + 1]
        for side, copy in enumerate(copies):
            copy.wait()
            for r in range(SLOTS):
                term = spread[SLOTS * (side + 1) + r] * rim_in[step, side, r : r + 1]
                sums[r % 4] = sums[r % 4] + term
        smooth = (sums[0] + sums[1]) + (sums[2] + sums[3])
    return smooth


def apply_weights(spread, own, below, above):
    sums = [jnp.zeros((8, 128), F32) for _ in range(4)]
    for i, rows in enumerate((own, below, above)):
        for r in range(SLOTS):
            sums[r % 4] = sums[r % 4] + spread[SLOTS * i + r] * rows[r : r + 1]
    return (sums[0] + sums[1]) + (sums[2] + sums[3])


def smooth_at_once(smooth, spread, rim_out, rim_in, send_sem, recv_sem):
    s, c = lax.axis_index("span"), lax.axis_index("cnn")
    rim_out[0] = smooth
    copies = [
        remote(rim_out.at[0], rim_in.at[i], send_sem.at[i], recv_sem.at[i], ((s + ahead) % 8, c))
        for i, ahead in enumerate((1, 7, 2, 6))
    ]
    for copy in copies:
        copy.start()
    for copy in copies:
        copy.wait()
    below, above, below2, above2 = [rim_in[i] for i in range(4)]
    own1 = apply_weights(spread.at[0], smooth, below, above)
    below1 = apply_weights(spread.at[1], below, below2, smooth)
    above1 = apply_weights(spread.at[2], above, smooth, above2)
    return apply_weights(spread.at[0], own1, below1, above1)


def to_logits(units, head):
    logits = lax.dot_general(
        units, head[...], (((1,), (1,)), ((), ())),
        preferred_element_type=F32, precision=lax.Precision.HIGHEST,
    )
    return jnp.concatenate([logits * (1.0 / VIEWS), jnp.zeros((8, 128 - CLASSES), F32)], axis=1)


def label_kernel(
    views, count, edges, bounds, patch_w, w1_h, w2_h, w3_h, w4_h, head,
    labels, more_out,
    w1, w2, w3, w4, own0, own_a, own_b, own_c, own_d, early, late, send,
    mine, x_in, c_mine, c_in, back_out, back_in, weight, weight_in, spread, rim_out, rim_in,
    sel, wp, w1p, w2p, m0, m1, m2, m3, m4, m5, m6, m7, m8, m9,
    own_sem, local_sem, weight_sem, view_send, view_recv,
    x_send, x_recv, c_send, c_recv, w_send, w_recv, b_send, b_recv, r_send, r_recv,
):
    net = (sel, wp, w1p, w2p, m0, m1, m2, m3, m4, m5, m6, m7, m8, m9)
    s, c = lax.axis_index("span"), lax.axis_index("cnn")
    near = neighbours()
    along_x = [((s + o) % 8, c) for o in range(1, 8)]
    along_c = [(s, (c + o) % 16) for o in range(1, 16)]
    barrier = pltpu.get_barrier_semaphore()
    for other in along_x + along_c:
        pl.semaphore_signal(barrier, inc=1, device_id=other, device_id_type=MESH)

    own = ((own_a, own_b), (own_c, own_d))
    copies = [
        pltpu.make_async_copy(
            views.at[pl.ds(1, SLOTS - 1), half * PAIR + j], own[half][j], local_sem.at[half, j]
        )
        for half in range(2)
        for j in range(PAIR)
    ]
    first_copies = [
        pltpu.make_async_copy(src, dst, weight_sem.at[i])
        for i, (src, dst) in enumerate(((w1_h, w1), (w2_h, w2), (w3_h, w3), (w4_h, w4)))
    ]
    first_copies.append(pltpu.make_async_copy(views.at[0], own0, own_sem))
    first_copies.insert(2, first_copies.pop())
    for copy in copies + first_copies:
        copy.start()

    own_count = count[0, 0]
    me = s * 16 + c
    lane = lax.broadcasted_iota(I32, (8, 128), 1)
    row = lax.broadcasted_iota(I32, (8, 128), 0)
    exported = [remainder(bounds[r], own_count, SLOTS) for r in range(RIM)]
    mine[...] = jnp.where(
        lane == me, jnp.where(row == 0, own_count, jnp.where(row == 1, exported[0], exported[1])), 0
    )
    x_copies = [
        remote(mine, x_in.at[o], x_send.at[o], x_recv.at[o], along_x[o]) for o in range(7)
    ]
    c_copies = [
        remote(c_mine, c_in.at[o], c_send.at[o], c_recv.at[o], along_c[o]) for o in range(15)
    ]

    divisor = jnp.maximum(own_count - 1, 1)
    slot = [jnp.int32(1) + lax.rem(jnp.int32(d), divisor) for d in range(DIRS)]
    early_copies, late_copies = [], []

    def fill(half, j, directions):
        for d in directions:
            for ch in range(4):
                send[half, j, d, ch] = own[half][j][jnp.clip(slot[d] - 1, 0, SLOTS - 2), ch]

    def pass_on(half, j, directions):
        for d in directions:
            if half == 0:
                target = early.at[j, BACK[d]]
            elif d == 0:
                target = early.at[j, DIRS]
            else:
                target = late.at[j, BACK[d] - 1]
            copy = remote(
                send.at[half, j, d], target, view_send.at[half, j, d], view_recv.at[half, j, BACK[d]], near[d]
            )
            copy.start()
            (late_copies if half and d else early_copies).append(copy)

    plan = {}

    def enter():
        pl.semaphore_wait(barrier, len(along_x) + len(along_c))
        for copy in x_copies:
            copy.start()

    def begin():
        copies[0].wait()
        fill(0, 0, range(DIRS))

    def counts_on():
        for copy in x_copies:
            copy.wait()
        counts = mine[...]
        for o in range(7):
            counts = counts + x_in[o]
        c_mine[...] = counts
        for copy in c_copies:
            copy.start()
        pass_on(0, 0, range(DIRS))

    def second_views():
        copies[1].wait()
        fill(0, 1, range(DIRS))
        pass_on(0, 1, range(DIRS))

    def second_halves():
        for j in range(PAIR):
            copies[PAIR + j].wait()
            fill(1, j, range(1))
            pass_on(1, j, range(1))

    def late_views(j):
        fill(1, j, range(1, DIRS))
        pass_on(1, j, range(1, DIRS))

    w_copies = [
        remote(weight, weight_in.at[i], w_send.at[i], w_recv.at[i], along_x[ahead - 1])
        for i, ahead in enumerate((1, 7))
    ]

    def planning():
        for copy in c_copies:
            copy.wait()
        counts = c_mine[...]
        for o in range(15):
            counts = counts + c_in[o]
        below = jnp.where(lane == lax.rem(me + 112, 128), counts, 0)
        above = jnp.where(lane == lax.rem(me + 16, 128), counts, 0)
        rims = [[jnp.sum(v[1 + r : 2 + r]) for r in range(RIM)] for v in (below, above)]
        weight[...] = smooth_weights(edges, own_count, *rims)
        for copy in w_copies:
            copy.start()
        for n, _ in enumerate(plan_steps(jnp.broadcast_to(counts[0:1], (8, 128)), plan)):
            if n % 3 == 2:
                yield

    def spreading():
        for i, tile in enumerate((weight, weight_in.at[0], weight_in.at[1])):
            spread_weights(tile[...], spread.at[i])
            yield

    enter()
    begin()
    counts_on()
    second_views()
    second_halves()
    late_views(0)
    late_views(1)
    for copy in first_copies[:2]:
        copy.wait()
    prepare(patch_w, w1, w2, *net)
    for copy in first_copies[2:]:
        copy.wait()

    units = []
    for half in range(2):
        loads = [
            lambda ch, first, rows, v=half * PAIR + j: own0[v, ch, pl.ds(first, rows), :]
            for j in range(PAIR)
        ]
        task = planning() if half else iter(())
        units.append(pair_feature(loads, w3, w4, *net, between=lambda task=task: next(task, None)))
        for _ in task:
            pass

    def here(v):
        return jnp.sum(jnp.where((lane == me)[0:1], v[0:1], 0))

    live = (jnp.left_shift(jnp.int32(1), own_count) - 1) & 254
    kept = [live & ~here(plan["passed"][half]) for half in range(2)]
    got = [here(plan["taken"][half]) for half in range(2)]
    mask = got[0] | ((got[1] & 1) << DIRS)
    mask = mask | ((kept[0] >> 1) << (OWN + 1)) | ((kept[1] >> 1) << (OWN_LATE + 1))
    picks = []
    for _ in range(GOAL):
        pick = lowest(mask, PLACES)
        picks.append(pick)
        last = jnp.where(pick >= 0, jnp.left_shift(jnp.int32(1), jnp.maximum(pick, 0)), 0)
        mask = mask & ~last
    third = picks[-1]
    late_dir = lowest(got[1] & ~1, DIRS)
    has_late = late_dir >= 0
    mask = mask | jnp.where(has_late, last, 0)
    picks[-1] = jnp.where(has_late, PLACES + late_dir, third)

    def at_place(place, j, ch, first, rows):
        pixels = [
            ref[jnp.clip(place - base, 0, most), ch, pl.ds(first, rows), :]
            for ref, base, most in (
                (early.at[j], 0, DIRS),
                (own[0][j], OWN + 1, SLOTS - 2),
                (own[1][j], OWN_LATE + 1, SLOTS - 2),
            )
        ]
        return jnp.where(
            place <= OWN, pixels[0], jnp.where(place <= OWN_LATE, pixels[1], pixels[2])
        )

    for copy in early_copies:
        copy.wait()
    for n in range(GOAL - 1):
        loads = [
            lambda ch, first, rows, j=j, n=n: at_place(picks[n], j, ch, first, rows)
            for j in range(PAIR)
        ]
        units.append(pair_feature(loads, w3, w4, *net))
    for copy in late_copies + w_copies:
        copy.wait()
    place_late = jnp.clip(late_dir - 1, 0, DIRS - 2)
    loads = [
        lambda ch, first, rows, j=j: jnp.where(
            has_late,
            late[j, place_late, ch, pl.ds(first, rows), :],
            at_place(third, j, ch, first, rows),
        )
        for j in range(PAIR)
    ]
    task = spreading()
    units.append(pair_feature(loads, w3, w4, *net, between=lambda: next(task, None)))

    logits = to_logits(jnp.concatenate(units + [jnp.zeros((8 - len(units), 256), F32)], axis=0), head)
    b_copies = []
    for d in range(DIRS):
        answer = jnp.zeros((8, 128), F32)
        for n, pick in enumerate(picks):
            ours = (pick == d) | (pick == PLACES + d)
            if d == 0:
                ours = ours | (pick == DIRS)
            answer = answer + jnp.where(ours, logits[2 + n : 3 + n], 0.0)
        back_out[d] = answer
        copy = remote(back_out.at[d], back_in.at[BACK[d]], b_send.at[d], b_recv.at[BACK[d]], near[d])
        copy.start()
        b_copies.append(copy)
    result = jnp.where(row == 0, logits[0:1] + logits[1:2], 0.0)
    for n, pick in enumerate(picks):
        for base in (OWN, OWN_LATE):
            is_own = (pick > base) & (pick < base + SLOTS) & (row == pick - base)
            result = result + jnp.where(is_own, logits[2 + n : 3 + n], 0.0)
    rest0 = (mask >> (OWN + 1)) & 127
    rest1 = (mask >> (OWN_LATE + 1)) & 127
    any_left = jnp.sum((plan["load"][0:1] > GOAL).astype(I32))
    more_out[2] = jnp.where(lane == 0, rest0 | (rest1 << 7), any_left).astype(F32)
    more_out[1] = weight[...]
    for copy in b_copies:
        copy.wait()
    for d in range(DIRS):
        result = result + jnp.where(row == slot[d], back_in[d], 0.0)
    result = jnp.where(row < own_count, result, 0.0)
    more_out[0] = result
    smooth = smooth_at_once(result, spread, rim_out, rim_in, r_send, r_recv)
    labels[...] = smooth[:, 0:CLASSES]


def label(views, count, edges, bounds, patch_w, w1, w2, w3, w4, head):
    dma = pltpu.SemaphoreType.DMA
    pixels = (4, 128, 256)
    tile = (8, 128)
    return pl.pallas_call(
        label_kernel,
        out_shape=(
            jax.ShapeDtypeStruct((SLOTS, CLASSES), F32),
            jax.ShapeDtypeStruct((3, *tile), F32),
        ),
        in_specs=[ANY, SMEM, SMEM, SMEM, VMEM, ANY, ANY, ANY, ANY, VMEM],
        out_specs=(VMEM, VMEM),
        scratch_shapes=[
            *[pltpu.VMEM(w.shape, BF) for w in (w1, w2, w3, w4)],
            pltpu.VMEM((VIEWS, *pixels), BF),
            *[pltpu.VMEM((SLOTS - 1, *pixels), BF)] * (2 * PAIR),
            pltpu.VMEM((PAIR, DIRS + 1, *pixels), BF),
            pltpu.VMEM((PAIR, DIRS - 1, *pixels), BF),
            pltpu.VMEM((2, PAIR, DIRS, *pixels), BF),
            pltpu.VMEM(tile, I32),
            pltpu.VMEM((7, *tile), I32),
            pltpu.VMEM(tile, I32),
            pltpu.VMEM((15, *tile), I32),
            pltpu.VMEM((DIRS, *tile), F32),
            pltpu.VMEM((DIRS, *tile), F32),
            pltpu.VMEM(tile, F32),
            pltpu.VMEM((2, *tile), F32),
            pltpu.VMEM((3, 3 * SLOTS, *tile), F32),
            pltpu.VMEM((1, *tile), F32),
            pltpu.VMEM((4, *tile), F32),
            *net_scratch(),
            dma(()), dma((2, PAIR)), dma((4,)),
            dma((2, PAIR, DIRS)), dma((2, PAIR, DIRS)),
            dma((7,)), dma((7,)), dma((15,)), dma((15,)), dma((2,)), dma((2,)),
            dma((DIRS,)), dma((DIRS,)), dma((4,)), dma((4,)),
        ],
        compiler_params=pltpu.CompilerParams(
            collective_id=0, has_side_effects=True, vmem_limit_bytes=58 << 20
        ),
    )(views, count, edges, bounds, patch_w, w1, w2, w3, w4, head)


def rest_kernel(
    left, views, patch_w, w1, w2, w3, w4, head, total,
    total_out, own, pw_v, w1_v, w2_v, w3_v, w4_v, *net_and_sems,
):
    net, sems = net_and_sems[:-1], net_and_sems[-1]
    mask = left[0, 0].astype(I32)
    total_out[...] = total[...]

    @pl.when(mask != 0)
    def _():
        moves = [
            pltpu.make_async_copy(a, b, sems.at[i])
            for i, (a, b) in enumerate(
                ((patch_w, pw_v), (w1, w1_v), (w2, w2_v), (w3, w3_v), (w4, w4_v))
            )
        ]
        for move in moves:
            move.start()
        for move in moves:
            move.wait()
        prepare(pw_v, w1_v, w2_v, *net)

        @pl.loop(0, 2 * (SLOTS - 1))
        def _(i):
            @pl.when((mask >> i) & 1 == 1)
            def _():
                slot, half = 1 + i % (SLOTS - 1), i // (SLOTS - 1)
                move = pltpu.make_async_copy(
                    views.at[slot, pl.ds(half * PAIR, PAIR)], own, sems.at[5]
                )
                move.start()
                move.wait()
                loads = [
                    lambda ch, first, rows, v=j: own[v, ch, pl.ds(first, rows), :]
                    for j in range(PAIR)
                ]
                unit = jnp.broadcast_to(pair_feature(loads, w3_v, w4_v, *net), (8, 256))
                logits = to_logits(unit, head)
                row = lax.broadcasted_iota(I32, (8, 128), 0)
                total_out[...] += jnp.where(row == slot, logits, 0.0)


def rest(left, views, patch_w, w1, w2, w3, w4, head, total):
    pixels = (4, 128, 256)
    return pl.pallas_call(
        rest_kernel,
        out_shape=jax.ShapeDtypeStruct((8, 128), F32),
        in_specs=[SMEM] + [ANY] * 6 + [VMEM] * 2,
        out_specs=VMEM,
        scratch_shapes=[
            pltpu.VMEM((PAIR, *pixels), BF),
            pltpu.VMEM(patch_w.shape, BF),
            pltpu.VMEM(w1.shape, BF),
            pltpu.VMEM(w2.shape, BF),
            pltpu.VMEM(w3.shape, BF),
            pltpu.VMEM(w4.shape, BF),
            *net_scratch(),
            pltpu.SemaphoreType.DMA((6,)),
        ],
        compiler_params=pltpu.CompilerParams(vmem_limit_bytes=58 << 20),
    )(left, views, patch_w, w1, w2, w3, w4, head, total)


def smooth_kernel(total, weight, labels, spread, rim_out, rim_in, send_sem, recv_sem):
    s, c = lax.axis_index("span"), lax.axis_index("cnn")
    barrier = pltpu.get_barrier_semaphore()
    for other in (((s + 1) % 8, c), ((s + 7) % 8, c)):
        pl.semaphore_signal(barrier, inc=1, device_id=other, device_id_type=MESH)
    spread_weights(weight[...], spread)
    pl.semaphore_wait(barrier, 2)
    smooth = smooth_steps(total[...], spread, rim_out, rim_in, send_sem, recv_sem)
    labels[...] = smooth[:, 0:CLASSES]


def smoothing(total, weight):
    dma = pltpu.SemaphoreType.DMA
    return pl.pallas_call(
        smooth_kernel,
        out_shape=jax.ShapeDtypeStruct((SLOTS, CLASSES), F32),
        in_specs=[VMEM, VMEM],
        out_specs=VMEM,
        scratch_shapes=[
            pltpu.VMEM((3 * SLOTS, 8, 128), F32),
            pltpu.VMEM((ITERS, 8, 128), F32),
            pltpu.VMEM((ITERS, 2, 8, 128), F32),
            dma((ITERS, 2)),
            dma((ITERS, 2)),
        ],
        compiler_params=pltpu.CompilerParams(collective_id=1, has_side_effects=True),
    )(total, weight)


def per_device(
    views, live_counts, skeleton_edges, boundary_rows,
    patch_weight, conv_first, conv_second, conv_third, conv_fourth, head_weight,
):
    weights = (
        patch_weight.reshape(64, 128),
        conv_first,
        conv_second,
        conv_third.reshape(1152, 256),
        conv_fourth.reshape(2304, 256),
        head_weight.T,
    )
    labels, more = label(views, live_counts, skeleton_edges.T, boundary_rows, *weights)

    def with_rest():
        return smoothing(rest(more[2], views, *weights, more[0]), more[1])

    return lax.cond(more[2, 0, 1] > 0, with_rest, lambda: labels)


def solution(mesh):
    placed = (
        P(("span", "cnn"), None, None, None, None),
        P("span", "cnn"),
        P(("span", "cnn"), None),
        P(("span", "cnn")),
        P(),
        P(),
        P(),
        P(),
        P(),
        P(),
    )
    return jax.shard_map(
        per_device, mesh=mesh, in_specs=placed, out_specs=P(("span", "cnn"), None), check_vma=False
    )
```
